32 devices in a mesh: rep: 4 (over y, x), seq: 8 (over z, core).
Axes of the slice: x: 2, y: 2, z: 4, core: 2. Of those that a mesh axis runs over, the one named last changes fastest.
Arguments:
- inputs: bfloat16 [196608, 512], P(('rep', 'seq'))
- mel_frames: bfloat16 [80, 196608], P(None, ('rep', 'seq')), may hold values from -6 to 6
- utterance: int32 [196608], P(('rep', 'seq')), may hold values from 0 to 15, never falling along the last dimension, each value on 1 to 49152 neighbouring positions
- keep_mask: int32 [196608], P(('rep', 'seq')), may hold values 0 or 1
- res_grad: bfloat16 [196608, 512], P(('rep', 'seq')), may hold values from -6 to 6
- skip_grad: bfloat16 [196608, 512], P(('rep', 'seq')), may hold values from -6 to 6
- conv_weight: float32 [512, 2, 1024], P('seq'), may hold values from -0.1875 to 0.1875
- cond_weight: float32 [80, 1024], P(None, 'seq'), may hold values from -0.625 to 0.625
- out_weight: float32 [512, 1024], P('seq'), may hold values from -0.25 to 0.25
- biases: float32 [2048], P('seq'), may hold values from -2 to 2
- conv_first: float32 [512, 2, 1024], P('seq')
- conv_second: float32 [512, 2, 1024], P('seq')
- cond_first: float32 [80, 1024], P(None, 'seq')
- cond_second: float32 [80, 1024], P(None, 'seq')
- out_first: float32 [512, 1024], P('seq')
- out_second: float32 [512, 1024], P('seq')
- bias_first: float32 [2048], P('seq')
- bias_second: float32 [2048], P('seq')
Outputs:
- residual_out: bfloat16 [196608, 512], P(('rep', 'seq'))
- skip_out: bfloat16 [196608, 512], P(('rep', 'seq'))
- input_grad: bfloat16 [196608, 512], P(('rep', 'seq'))
- grad_norm: float32 [], replicated
- conv_first_new: float32 [512, 2, 1024], P('seq')
- conv_second_new: float32 [512, 2, 1024], P('seq')
- conv_weight_new: float32 [512, 2, 1024], P('seq')
- cond_first_new: float32 [80, 1024], P(None, 'seq')
- cond_second_new: float32 [80, 1024], P(None, 'seq')
- cond_weight_new: float32 [80, 1024], P(None, 'seq')
- out_first_new: float32 [512, 1024], P('seq')
- out_second_new: float32 [512, 1024], P('seq')
- out_weight_new: float32 [512, 1024], P('seq')
- bias_first_new: float32 [2048], P('seq')
- bias_second_new: float32 [2048], P('seq')
- bias_new: float32 [2048], P('seq')
The draws below stay inside these ranges and needn't reach their ends.
Inputs may be any that keep to these rules, and one draw needn't show every extreme that they name: utterance never falls along time; every number below the count occurs; one utterance has exactly 49152 samples.
All inputs are finite; a program needn't handle non-finite values. No bound on the sum of `keep_mask` on one device may be relied on, other than what follows from the above.
Results may differ from the reference program's by a relative error of at most 0.007.
Values may be sent and summed in bfloat16 or wider, within the bound.
No kernel may reach another device: no remote copies, remote signals or barrier semaphores. Data moves between devices by JAX's collectives and lax.ppermute only.
A program may use at most 256 MiB of HBM per device.

```python
import math
import jax
import jax.numpy as jnp
import numpy as np
from jax import lax

RESIDUAL_WIDTH = 512
G = 1024
S = 512
C = 80
DILATION_STEP = 512
STEP = 10
TOK_DEV = 6144
TOKENS = 196608
BIAS = 2048
N_SEQ = 8


def entry_size(kind_rms):
    total = 2 * RESIDUAL_WIDTH * G * 0.36 + C * G * 0.09 + G // 2 * (RESIDUAL_WIDTH + S) * 0.2 + (G + RESIDUAL_WIDTH + S) * 0.36
    return kind_rms / math.sqrt(total)


def first_moment(key, shape, kind_rms):
    return jax.random.normal(key, shape, jnp.float32) * (0.111 * entry_size(kind_rms))


def second_moment(key, shape, kind_rms):
    spread = jnp.exp(jax.random.uniform(key, shape, jnp.float32, 0.0, math.log(4.0)))
    return spread * (0.001 * entry_size(kind_rms) ** 2)


def draw_inputs(key, part):
    key = jax.random.fold_in(key, 3)
    column = jnp.arange(RESIDUAL_WIDTH, dtype=jnp.float32) / (RESIDUAL_WIDTH - 1)
    base = jax.random.normal(key, (TOKENS, RESIDUAL_WIDTH), jnp.float32)
    ramp = jnp.power(3.0, column)
    return (base * ramp[None, :]).astype(jnp.bfloat16)


def draw_conv_first(key, part):
    key = jax.random.fold_in(key, 11)
    return first_moment(key, (RESIDUAL_WIDTH, 2, G), 0.6)


def draw_conv_second(key, part):
    key = jax.random.fold_in(key, 12)
    return second_moment(key, (RESIDUAL_WIDTH, 2, G), 0.6)


def draw_cond_first(key, part):
    key = jax.random.fold_in(key, 13)
    return first_moment(key, (C, G), 0.3)


def draw_cond_second(key, part):
    key = jax.random.fold_in(key, 14)
    return second_moment(key, (C, G), 0.3)


def draw_out_first(key, part):
    key = jax.random.fold_in(key, 15)
    return first_moment(key, (G // 2, RESIDUAL_WIDTH + S), 0.45)


def draw_out_second(key, part):
    key = jax.random.fold_in(key, 16)
    return second_moment(key, (G // 2, RESIDUAL_WIDTH + S), 0.45)


def draw_bias_first(key, part):
    key = jax.random.fold_in(key, 17)
    return first_moment(key, (G + RESIDUAL_WIDTH + S,), 0.6)


def draw_bias_second(key, part):
    key = jax.random.fold_in(key, 18)
    return second_moment(key, (G + RESIDUAL_WIDTH + S,), 0.6)


def touch_ends(entries, rng, least, largest):
    place = [jax.random.randint(jax.random.fold_in(rng, axis), (), 0, length) for axis, length in enumerate(entries.shape)]
    main_axis = entries.shape.index(max(entries.shape))
    beside = place[:main_axis] + [(place[main_axis] + 1) % entries.shape[main_axis]] + place[main_axis + 1:]
    return entries.at[tuple(place)].set(least).at[tuple(beside)].set(largest)


def block_levels(key, extent, cuts, smallest, top_value):
    def one(position, shards_of):
        heights = jax.random.uniform(jax.random.fold_in(jax.random.fold_in(key, 6), position), (shards_of,), jnp.float32, smallest / len(cuts), top_value / len(cuts))
        return jnp.repeat(jnp.exp(heights), extent[position] // shards_of).reshape((-1,) + (1,) * (len(extent) - position - 1))

    level = one(*cuts[0])
    for cut in cuts[1:]:
        level = level * one(*cut)
    return level


def length_profile(amount, total, reach, slope):
    weights = [(1 << 20) // math.isqrt(grade ** slope) + 1 for grade in range(2, amount + 1)]
    surplus, counts = total - reach - (amount - 1), [1] * (amount - 1)
    while surplus > 0:
        free = [i for i in range(amount - 1) if counts[i] < reach]
        pool, budget = sum([weights[i] for i in free]), surplus
        for i in free:
            extra = min(reach - counts[i], max(1, budget * weights[i] // pool), surplus)
            counts[i] = counts[i] + extra
            surplus = surplus - extra
    return np.array([reach] + counts)


def ragged_sizes(rng, amount, total, most, slope):
    if amount == 2:
        one = jax.random.randint(rng, (), max(1, total - most), min(most, total - 1) + 1)
        return jnp.stack([one, total - one])
    lengths = jnp.asarray(length_profile(amount, total, most, slope), jnp.int32)
    pairs = (amount - 1) // 2
    source_of, taker = lengths[1:1 + 2 * pairs:2], lengths[2:2 + 2 * pairs:2]
    slack = jnp.minimum(source_of - 1, most - taker)
    moved = jax.random.randint(jax.random.fold_in(rng, 1), (pairs,), 0, 1 << 20) % (slack + 1)
    lengths = lengths.at[1:1 + 2 * pairs:2].set(source_of - moved).at[2:2 + 2 * pairs:2].set(taker + moved)
    return lengths[jax.random.permutation(jax.random.fold_in(rng, 2), amount)]


def scatter_about(own_key, dims, scale, most, shards=(), held_as=jnp.bfloat16):
    entries = jax.random.normal(own_key, dims, jnp.float32) * scale
    if len(shards) > 0:
        entries = block_levels(own_key, dims, shards, -0.22, 0.18) * entries
    return jnp.clip(entries, min=-most, max=most).astype(held_as)


def setup_inputs(seed: int = 0) -> dict:
    arg_keys = jax.random.split(jax.random.key(seed), 19)
    return {
        "inputs": draw_inputs(jax.random.fold_in(arg_keys[18], 71), 0),
        "mel_frames": scatter_about(arg_keys[1], (C, TOKENS), 1.0, 6.0, ((1, 32),)),
        "utterance": jnp.searchsorted(jnp.cumsum(ragged_sizes(arg_keys[2], TOKENS // (2 * TOK_DEV), TOKENS, TOK_DEV * N_SEQ, 0)), jnp.arange(TOKENS), side="right").astype(jnp.int32),
        "keep_mask": touch_ends((jax.random.randint(arg_keys[3], (TOKENS,), 0, 8) < 7).astype(jnp.int32), jax.random.fold_in(arg_keys[3], 1), 0, 1),
        "res_grad": scatter_about(arg_keys[4], (TOKENS, RESIDUAL_WIDTH), 1.0, 6.0, ((0, 32),)),
        "skip_grad": scatter_about(arg_keys[5], (TOKENS, S), 1.0, 6.0, ((0, 32),)),
        "conv_weight": scatter_about(arg_keys[6], (RESIDUAL_WIDTH, 2, G), (2 * RESIDUAL_WIDTH) ** -0.5, 0.1875, ((0, 8),), jnp.float32),
        "cond_weight": scatter_about(arg_keys[7], (C, G), C ** -0.5, 0.625, ((1, 8),), jnp.float32),
        "out_weight": scatter_about(arg_keys[8], (G // 2, RESIDUAL_WIDTH + S), (G // 2) ** -0.5, 0.25, ((0, 8),), jnp.float32),
        "biases": scatter_about(arg_keys[9], (BIAS,), 0.3, 2.0, ((0, 8),), jnp.float32),
        "conv_first": draw_conv_first(jax.random.fold_in(arg_keys[18], 71), 0),
        "conv_second": draw_conv_second(jax.random.fold_in(arg_keys[18], 71), 0),
        "cond_first": draw_cond_first(jax.random.fold_in(arg_keys[18], 71), 0),
        "cond_second": draw_cond_second(jax.random.fold_in(arg_keys[18], 71), 0),
        "out_first": draw_out_first(jax.random.fold_in(arg_keys[18], 71), 0),
        "out_second": draw_out_second(jax.random.fold_in(arg_keys[18], 71), 0),
        "bias_first": draw_bias_first(jax.random.fold_in(arg_keys[18], 71), 0),
        "bias_second": draw_bias_second(jax.random.fold_in(arg_keys[18], 71), 0),
    }


beta_one = 0.9
beta_two = 0.999
learn_rate = 0.05
weight_decay = 0.01
epsilon = 1e-08
clip_bound = 1.0

@jax.custom_vjp
def low(v):
    return lax.optimization_barrier(v.astype(jnp.bfloat16)).astype(jnp.float32)

@jax.custom_vjp
def low_back(v):
    return v

def low_keep(v):
    return (low(v), None)

def low_pass(kept, grad):
    return (grad,)

def back_keep(v):
    return (v, None)

def back_low(kept, grad):
    return (low(grad),)
low.defvjp(low_keep, low_pass)
low_back.defvjp(back_keep, back_low)

def highest(left, right):
    return jnp.dot(left, right, precision=lax.Precision.HIGHEST)

def block_out(weights, pieces):
    conv_low, cond_low, out_low, bias_low = weights
    rows_in, rows_early, mel_block, keep_block = pieces
    pre = highest(rows_in, conv_low[:, 0, :]) + highest(rows_early, conv_low[:, 1, :])
    pre = pre + jnp.einsum('ct,cg->tg', mel_block, cond_low, precision=lax.Precision.HIGHEST) + bias_low[:G]
    pre = low_back(pre)
    filt = jnp.tanh(pre[:, :G // 2])
    gate = jax.nn.sigmoid(pre[:, G // 2:])
    hidden = low(keep_block[:, None] * filt * gate)
    mixed = highest(hidden, out_low) + bias_low[G:]
    return (rows_in + mixed[:, :RESIDUAL_WIDTH], mixed[:, RESIDUAL_WIDTH:])

def forward(input_float, mels_f, conv_weight, cond_weight, out_weight, biases, joined_pairs, keep_f):
    weights = (low(conv_weight), low(cond_weight), low(out_weight), low(biases))
    preceding_rows = jnp.concatenate([jnp.zeros((DILATION_STEP, RESIDUAL_WIDTH), jnp.float32), input_float[:-DILATION_STEP]], 0) * joined_pairs[:, None]
    blocks = TOKENS // TOK_DEV
    pieces = (input_float.reshape(blocks, TOK_DEV, RESIDUAL_WIDTH), preceding_rows.reshape(blocks, TOK_DEV, RESIDUAL_WIDTH), mels_f.reshape(C, blocks, TOK_DEV).transpose(1, 0, 2), keep_f.reshape(blocks, TOK_DEV))
    checked = jax.checkpoint(block_out)
    residual, skip = lax.map(lambda piece: checked(weights, piece), pieces)
    return (residual.reshape(TOKENS, RESIDUAL_WIDTH), skip.reshape(TOKENS, S))

def adamw_update(grad, moment, second, weight, factor, decay):
    clipped = grad * factor
    moment_new = beta_one * moment + (1.0 - beta_one) * clipped
    second_new = beta_two * second + (1.0 - beta_two) * clipped * clipped
    mean_hat = moment_new / (1.0 - beta_one ** STEP)
    square_hat = second_new / (1.0 - beta_two ** STEP)
    weight_new = weight - learn_rate * (mean_hat / (jnp.sqrt(square_hat) + epsilon) + decay * weight)
    return (moment_new, second_new, weight_new)

def reference(inputs, mel_frames, utterance, keep_mask, res_grad, skip_grad, conv_weight, cond_weight, out_weight, biases, conv_first, conv_second, cond_first, cond_second, out_first, out_second, bias_first, bias_second):
    input_float = inputs.astype(jnp.float32)
    mels_f = mel_frames.astype(jnp.float32)
    preceding_index = jnp.concatenate([jnp.full((DILATION_STEP,), -1, jnp.int32), utterance[:-DILATION_STEP].astype(jnp.int32)], 0)
    joined_pairs = (preceding_index == utterance.astype(jnp.int32)).astype(jnp.float32)
    keep_f = keep_mask.astype(jnp.float32)

    def run(inputs_v, conv_v, cond_v, out_v, bias_v):
        return forward(inputs_v, mels_f, conv_v, cond_v, out_v, bias_v, joined_pairs, keep_f)
    (residual, skip), pull = jax.vjp(run, input_float, conv_weight, cond_weight, out_weight, biases)
    input_grad, grad_conv, grad_cond, grad_out, grad_bias = pull((res_grad.astype(jnp.float32), skip_grad.astype(jnp.float32)))
    total = jnp.sum(grad_conv * grad_conv) + jnp.sum(grad_cond * grad_cond) + jnp.sum(grad_out * grad_out) + jnp.sum(grad_bias * grad_bias)
    grad_norm = jnp.sqrt(total)
    factor = clip_bound / jnp.maximum(grad_norm, clip_bound)
    conv_new = adamw_update(grad_conv, conv_first, conv_second, conv_weight, factor, weight_decay)
    cond_new = adamw_update(grad_cond, cond_first, cond_second, cond_weight, factor, weight_decay)
    out_new = adamw_update(grad_out, out_first, out_second, out_weight, factor, weight_decay)
    bias_new = adamw_update(grad_bias, bias_first, bias_second, biases, factor, 0.0)
    return (residual.astype(jnp.bfloat16), skip.astype(jnp.bfloat16), input_grad.astype(jnp.bfloat16), grad_norm, conv_new[0], conv_new[1], conv_new[2], cond_new[0], cond_new[1], cond_new[2], out_new[0], out_new[1], out_new[2], bias_new[0], bias_new[1], bias_new[2])
```

```python
import functools

import jax
import jax.numpy as jnp
from jax import lax
from jax.experimental import pallas as pl
from jax.experimental.pallas import tpu as pltpu
from jax.sharding import PartitionSpec as P

DILATION_STEP = 512
STEP = 10

beta_one = 0.9
beta_two = 0.999
learn_rate = 0.05
weight_decay = 0.01
epsilon = 1e-08
clip_bound = 1.0

LANES = 128
TILE = 16
AUX = 128
MEL = 80
ONES = 80
KEEP = 81
LINK = 82
ROWS = 512
BF = jnp.bfloat16
F32 = jnp.float32
BOTH = ("rep", "seq")


def from_behind(x, axis, by):
    count = lax.axis_size(axis)
    pairs = [(i, i + by) for i in range(count) if 0 <= i + by < count]
    return lax.ppermute(x, axis, pairs)


def swap(x, rep_bits, seq_bits):
    reps, seqs = lax.axis_size("rep"), lax.axis_size("seq")
    pairs = [
        (r * seqs + s, (r ^ rep_bits) * seqs + (s ^ seq_bits))
        for r in range(reps)
        for s in range(seqs)
    ]
    return lax.ppermute(x, BOTH, pairs)


def nt_dot(left, right):
    return lax.dot_general(
        left, right, (((1,), (1,)), ((), ())), preferred_element_type=F32
    )


def tn_dot(left, right):
    return lax.dot_general(
        left, right, (((0,), (0,)), ((), ())), preferred_element_type=F32
    )


def dot(left, right):
    return jnp.dot(left, right, preferred_element_type=F32)


def params(**more):
    return pltpu.CompilerParams(vmem_limit_bytes=58 * 2**20, **more)


def cost(flops, moved):
    return pl.CostEstimate(flops=int(flops), bytes_accessed=int(moved), transcendentals=0)


def whole(shape):
    return pl.BlockSpec(shape, lambda *_: (0,) * len(shape))


HEAD = 96
QUARTER = 3 * 8 * TILE


def pack_body(where, conv, out, cond, bias, own, first):
    own[0:MEL, :] = cond[...].astype(BF)
    own[MEL:HEAD, :] = jnp.concatenate(
        [bias[...], jnp.zeros((HEAD - MEL - 2, LANES), F32)], 0
    ).astype(BF)
    for k in range(4):
        start = pl.multiple_of((where[1] ^ k) * TILE, TILE)
        base = HEAD + k * QUARTER
        parts = (
            conv[0, pl.ds(start, TILE), :],
            conv[1, pl.ds(start, TILE), :],
            out[pl.ds(start, TILE), :].astype(BF),
        )
        for t, part in enumerate(parts):
            for j in range(8):
                own[pl.ds(base + t * 128 + j * TILE, TILE), :] = part[:, j * LANES : (j + 1) * LANES]
    first[...] = own[0 : HEAD + QUARTER, :]


def pack_weights(where, conv, out, cond, bias):
    spec = pl.BlockSpec(memory_space=pltpu.VMEM)
    return pl.pallas_call(
        pack_body,
        in_specs=[pl.BlockSpec(memory_space=pltpu.SMEM)] + [spec] * 4,
        out_specs=[spec, spec],
        out_shape=[
            jax.ShapeDtypeStruct((HEAD + 4 * QUARTER, LANES), BF),
            jax.ShapeDtypeStruct((HEAD + QUARTER, LANES), BF),
        ],
        compiler_params=params(),
        name="pack_weights",
    )(where, conv, out, cond, bias)


def mixed_block(block):
    low, mid, top = block & 1, (block >> 1) & 1, (block >> 2) & 1
    return low + 4 * mid + 2 * top


def unpack_body(where, *refs):
    owns, stacks, sides = refs[0:2], refs[2:4], (refs[4:7], refs[7:10])
    w, o, bias_out = refs[10:13]
    w[1120:1152, :] = jnp.zeros((32, w.shape[1]), BF)
    blank = jnp.zeros((TILE - 1, LANES), BF)
    for c in range(2):
        for j in range(4):
            shard = 2 * (where[2] ^ j) + (where[0] ^ c)
            small = owns[c][0:HEAD, :] if j == 0 else stacks[c][j - 1, 0:HEAD, :]
            lane = pl.multiple_of(mixed_block(shard) * LANES, LANES)
            w[1024 : 1024 + MEL, pl.ds(lane, LANES)] = small[0:MEL]
            tail = small[MEL:HEAD]

            @pl.when(shard < 4)
            def _():
                for e in range(2):
                    at = pl.multiple_of(mixed_block(2 * shard + e) * LANES, LANES)
                    w[1104:1120, pl.ds(at, LANES)] = jnp.concatenate([tail[e : e + 1], blank], 0)

            @pl.when(shard >= 4)
            def _():
                for e in range(2):
                    at = pl.multiple_of((2 * (shard - 4) + e) * LANES, LANES)
                    bias_out[:, pl.ds(at, LANES)] = jnp.broadcast_to(
                        tail[e : e + 1].astype(F32), (8, LANES)
                    )

            for k in range(4):
                row = pl.multiple_of(64 * shard + TILE * (where[1] ^ k), TILE)
                if j == 0:
                    source = owns[c].at[pl.ds(HEAD + k * QUARTER, QUARTER), :]
                elif k == 0:
                    source = stacks[c].at[j - 1, pl.ds(HEAD, QUARTER), :]
                else:
                    source = sides[c][k - 1].at[pl.ds((j - 1) * QUARTER, QUARTER), :]
                for b in range(8):
                    lanes = pl.ds(mixed_block(b) * LANES, LANES)
                    w[pl.ds(row, TILE), lanes] = source[b * TILE : (b + 1) * TILE, :]
                    w[pl.ds(512 + row, TILE), lanes] = source[128 + b * TILE : 128 + (b + 1) * TILE, :]
                    o[pl.ds(row, TILE), b * LANES : (b + 1) * LANES] = source[
                        256 + b * TILE : 256 + (b + 1) * TILE, :
                    ]


def gather_quarters(where, conv, out, cond, bias):
    own, first = pack_weights(where, conv, out, cond, bias)
    own_other = swap(own, 0, 1)
    along = [swap(first, 0, 2 * j) for j in (1, 2, 3)]
    stack = jnp.stack(along, 0)
    send = stack[:, HEAD:, :].reshape(3 * QUARTER, LANES)
    across = [swap(send, k, 0) for k in (1, 2, 3)]
    stack_other = swap(stack, 0, 1)
    across_other = [swap(a, 0, 1) for a in across]
    spec = pl.BlockSpec(memory_space=pltpu.VMEM)
    return pl.pallas_call(
        unpack_body,
        in_specs=[pl.BlockSpec(memory_space=pltpu.SMEM)] + [spec] * 10,
        out_specs=[spec] * 3,
        out_shape=[
            jax.ShapeDtypeStruct((1024 + AUX, 1024), BF),
            jax.ShapeDtypeStruct((512, 1024), BF),
            jax.ShapeDtypeStruct((8, 1024), F32),
        ],
        compiler_params=params(),
        name="unpack_weights",
    )(where, own, own_other, stack, stack_other, *across, *across_other)


def mixed_columns(x):
    rows, columns = x.shape
    return x.reshape(rows, 2, 2, columns // 4).transpose(0, 2, 1, 3).reshape(rows, columns)


def gather_plain(conv, out_weight, cond_weight, biases):
    conv_all = lax.all_gather(conv, "seq", axis=1, tiled=True)
    cond_all = lax.all_gather(cond_weight.astype(BF), "seq", axis=1, tiled=True)
    out_all = lax.all_gather(out_weight.astype(BF), "seq", axis=0, tiled=True)
    bias_all = lax.all_gather(biases.astype(BF), "seq", axis=0, tiled=True)
    gates = cond_all.shape[1]
    w = jnp.concatenate(
        [
            conv_all[0],
            conv_all[1],
            cond_all,
            bias_all[None, :gates],
            jnp.zeros((AUX - MEL - 1, gates), BF),
        ],
        0,
    )
    bias_out = jnp.broadcast_to(bias_all[None, gates:].astype(F32), (8, gates))
    return mixed_columns(w), out_all, bias_out


def fill_window(xe, x, tail, aux, carry, first):
    rows = x.shape[0]

    @pl.when(first)
    def _():
        carry[...] = tail[...]

    side = aux[...].T
    link = side[:, LINK : LINK + 1]
    xe[:, 0:512] = x[...]
    xe[0:ROWS, 512:1024] = carry[...] * link[0:ROWS]
    if rows > ROWS:
        xe[ROWS:, 512:1024] = x[0 : rows - ROWS, :] * link[ROWS:]
    xe[:, 1024:1152] = side
    carry[...] = x[rows - ROWS :, :]
    return side[:, KEEP : KEEP + 1].astype(F32), link.astype(F32)


def gated(xe, w, o, res, skp, keep):
    half = o.shape[0]
    pre = dot(xe[...], w[...])
    hg = nt_dot(res[...], o[:, 0:512]) + nt_dot(skp[...], o[:, 512:1024])
    filt = jnp.tanh(pre[:, :half])
    gate = 0.5 * jnp.tanh(0.5 * pre[:, half:]) + 0.5
    kept = keep * gate
    hidden = filt * kept
    filt_grad = hg * kept * (1.0 - filt * filt)
    gate_grad = hg * hidden * (1.0 - gate)
    return hidden.astype(BF), jnp.concatenate([filt_grad, gate_grad], 1).astype(BF)


def emit_pieces(where, keep_out, send_out, write):
    for c, dest in ((0, keep_out), (1, send_out)):

        def one(n, carry, c=c, dest=dest):
            k, j = n // 4, n % 4
            shard = 2 * (where[2] ^ j) + (where[0] ^ c)
            write(dest.at[k, j], shard, where[1] ^ k)
            return carry

        lax.fori_loop(0, 16, one, 0)


def put_tiles(dest, base, value):
    value = value.astype(dest.dtype)
    for b in range(value.shape[1] // LANES):
        dest[pl.ds(base + b * TILE, TILE), :] = value[:, b * LANES : (b + 1) * LANES]


def conv_piece(dest, acc, shard, quarter):
    row = pl.multiple_of(64 * shard + TILE * quarter, TILE)
    put_tiles(dest, 0, acc[pl.ds(row, TILE), :])
    put_tiles(dest, 64, acc[pl.ds(512 + row, TILE), :])


def first_body(split, where, x, tail, aux, res, skp, w, o, p, hid, *rest):
    if split:
        keep_out, send_out, aux_grad, sums, xe, carry, acc = rest
    else:
        grad, sums, xe, carry, acc = rest
    step, last = pl.program_id(0), pl.num_programs(0) - 1
    keep, _ = fill_window(xe, x, tail, aux, carry, step == 0)

    @pl.when(step == 0)
    def _():
        acc[...] = jnp.zeros_like(acc)
        sums[...] = jnp.zeros_like(sums)

    hidden, grad_pre = gated(xe, w, o, res, skp, keep)
    hid[...] = hidden
    p[...] = grad_pre
    acc[...] += tn_dot(xe[...], grad_pre)
    for n, part in enumerate((res, skp)):
        total = jnp.sum(part[...].astype(F32), 0, keepdims=True)
        sums[:, n * 512 : (n + 1) * 512] += jnp.broadcast_to(total, (8, 512))

    @pl.when(step == last)
    def _():
        if split:
            aux_grad[...] = acc[1024:1152, :]
            emit_pieces(
                where,
                keep_out,
                send_out,
                lambda dest, shard, quarter: conv_piece(dest, acc, shard, quarter),
            )
        else:
            grad[...] = acc[...]


def second_body(split, where, x, tail, aux, res, skp, w, o, hid_one, p_one, w_past, *rest):
    if split:
        aux_one, sums = rest[:2]
        p, hid, edge, keep_out, send_out, xe, carry, acc, acc_out, small = rest[2:]
    else:
        p, hid, edge, grad, grad_out, xe, carry, acc, acc_out = rest
    step, last = pl.program_id(0), pl.num_programs(0) - 1
    middle = pl.num_programs(0) // 2
    keep, link = fill_window(xe, x, tail, aux, carry, step == 0)

    @pl.when(step == 0)
    def _():
        acc[...] = jnp.zeros_like(acc)
        acc_out[...] = jnp.zeros_like(acc_out)

    hidden, grad_pre = gated(xe, w, o, res, skp, keep)
    hid[...] = hidden
    p[...] = grad_pre
    acc[...] += tn_dot(xe[...], grad_pre)
    both = jnp.concatenate([hid_one[...], hidden], 1)
    acc_out[:, 0:512] += tn_dot(both, res[...])
    acc_out[:, 512:1024] += tn_dot(both, skp[...])

    @pl.when((step == 0) | (step == middle))
    def _():
        cut = w.shape[1]
        past = nt_dot(p_one[...], w_past[...]) + nt_dot(p[0:ROWS, :], w[512:1024, :])
        edge[...] = (past * link[0:ROWS]).astype(BF)[None]

    @pl.when(step == last)
    def _():
        if not split:
            grad[...] = acc[...]
            grad_out[...] = acc_out[...]
            return
        small[...] = jnp.zeros_like(small)
        for s in range(8):
            block = mixed_block(s)
            source = aux_one if block < 4 else acc.at[pl.ds(1024, AUX), :]
            lane = (block % 4) * LANES
            small[s, 0:MEL, :] = source[0:MEL, lane : lane + LANES]
            for e in range(2):
                if s < 4:
                    block = mixed_block(2 * s + e)
                    source = aux_one if block < 4 else acc.at[pl.ds(1024, AUX), :]
                    lane = (block % 4) * LANES
                    line = source[ONES : ONES + 1, lane : lane + LANES]
                else:
                    lane = (2 * (s - 4) + e) * LANES
                    line = sums[0:1, lane : lane + LANES]
                small[s, MEL + e : MEL + e + 1, :] = line

        def write(dest, shard, quarter):
            conv_piece(dest, acc, shard, quarter)
            row = pl.multiple_of(64 * shard + TILE * quarter, TILE)
            put_tiles(dest, 128, acc_out[pl.ds(row, TILE), :])
            dest[256:288, :] = small[shard, pl.ds(pl.multiple_of(32 * quarter, 32), 32), :].astype(
                dest.dtype
            )

        emit_pieces(where, keep_out, send_out, write)


def half_layer(number, split, rows, where, x, tail, aux, res, skp, w, o, extra):
    total = x.shape[0]
    half = o.shape[0] // 2
    wide = 2 * half
    by_row = lambda columns: pl.BlockSpec((rows, columns), lambda i: (i, 0))
    steps = total // rows
    in_specs = [
        pl.BlockSpec(memory_space=pltpu.SMEM),
        by_row(512),
        whole((ROWS, 512)),
        pl.BlockSpec((AUX, rows), lambda i: (0, i)),
        by_row(512),
        by_row(512),
        pl.BlockSpec((1024 + AUX, wide), lambda i: (0, number)),
        pl.BlockSpec((half, 1024), lambda i: (number, 0)),
    ]
    out_specs = [by_row(wide), by_row(half)]
    out_shape = [
        jax.ShapeDtypeStruct((total, wide), BF),
        jax.ShapeDtypeStruct((total, half), BF),
    ]
    scratch = [
        pltpu.VMEM((rows, 1024 + AUX), BF),
        pltpu.VMEM((ROWS, 512), BF),
        pltpu.VMEM((1024 + AUX, wide), F32),
    ]
    units = 2.5 / 2 + 0.5 + 1.125

    def add_out(shape, dtype):
        out_specs.append(whole(shape))
        out_shape.append(jax.ShapeDtypeStruct(shape, dtype))

    if number == 0:
        body = first_body
        if split:
            add_out((4, 4, 128, LANES), F32)
            add_out((4, 4, 128, LANES), BF)
            add_out((AUX, wide), F32)
        else:
            add_out((1024 + AUX, wide), F32)
        add_out((8, 1024), F32)
    else:
        body = second_body
        units += 1
        middle = steps // 2
        in_specs += [
            by_row(half),
            pl.BlockSpec((ROWS, wide), lambda i: (jnp.where(i < middle, 0, middle * (rows // ROWS)), 0)),
            pl.BlockSpec((512, wide), lambda i: (1, 0)),
        ]
        if split:
            in_specs += [whole((AUX, wide)), whole((8, 1024))]
        out_specs.append(pl.BlockSpec((1, ROWS, 512), lambda i: (jnp.where(i < middle, 0, 1), 0, 0)))
        out_shape.append(jax.ShapeDtypeStruct((2, ROWS, 512), BF))
        if split:
            add_out((4, 4, 288, LANES), F32)
            add_out((4, 4, 288, LANES), BF)
        else:
            add_out((1024 + AUX, wide), F32)
            add_out((512, 1024), F32)
        scratch.append(pltpu.VMEM((512, 1024), F32))
        if split:
            scratch.append(pltpu.VMEM((8, AUX, LANES), F32))
    return pl.pallas_call(
        functools.partial(body, split),
        grid=(steps,),
        in_specs=in_specs,
        out_specs=out_specs,
        out_shape=out_shape,
        scratch_shapes=scratch,
        compiler_params=params(),
        cost_estimate=cost(units * 2 * total * 512 * 1024, total * 6000),
        name="half_layer_%d" % number,
    )(where, x, tail, aux, res, skp, w, o, *extra)


def mixed_body(x, one, two, o, bias, residual, skip):
    half = one.shape[1]
    mixed = dot(one[...], o[0:half, :]) + dot(two[...], o[half:, :]) + bias[0:1, :]
    residual[...] = (x[...].astype(F32) + mixed[:, 0:512]).astype(BF)
    skip[...] = mixed[:, 512:1024].astype(BF)


def mixed_layer(rows, x, one, two, o, bias):
    total, half = one.shape
    by_row = lambda columns: pl.BlockSpec((rows, columns), lambda i: (i, 0))
    return pl.pallas_call(
        mixed_body,
        grid=(total // rows,),
        in_specs=[by_row(512), by_row(half), by_row(half), whole((512, 1024)), whole((8, 1024))],
        out_specs=[by_row(512), by_row(512)],
        out_shape=[jax.ShapeDtypeStruct((total, 512), BF)] * 2,
        compiler_params=params(),
        cost_estimate=cost(2 * total * 512 * 1024, total * 4096),
        name="mixed_layer",
    )(x, one, two, o, bias)


def input_body(res, one, two, flags, w, edge, *rest):
    out, carry = rest[-2:]
    step = pl.program_id(0)
    rows = res.shape[0]
    wide = one.shape[1]

    @pl.when(step == 0)
    def _():
        carry[...] = edge[0]

    link = flags[...].T[:, LINK - MEL : LINK - MEL + 1].astype(F32)
    both = nt_dot(one[...], w[:, 0:wide]) + nt_dot(two[...], w[:, wide:])
    past = both[:, 512:1024] * link
    now = res[...].astype(F32) + both[:, 0:512]
    if rows > ROWS:
        out[0 : rows - ROWS, :] = (now[0 : rows - ROWS] + past[ROWS:]).astype(BF)
    out[rows - ROWS :, :] = (now[rows - ROWS :] + carry[...].astype(F32)).astype(BF)
    carry[...] = past[0:ROWS].astype(BF)


def input_layer(rows, part, parts, res, one, two, aux, w, edge, number, partial):
    total, wide = one.shape
    steps = total // rows // parts
    at = lambda i: steps * (part + 1) - 1 - i
    by_row = lambda columns: pl.BlockSpec((rows, columns), lambda i: (at(i), 0))
    in_specs = [
        by_row(512),
        by_row(wide),
        by_row(wide),
        pl.BlockSpec((TILE, rows), lambda i: (MEL // TILE, at(i))),
        pl.BlockSpec((1024, 2 * wide), lambda i: (0, 0)),
        pl.BlockSpec((1, ROWS, 512), lambda i: (number, 0, 0)),
    ]
    operands = [res, one, two, aux, w, edge]
    aliases = {}
    if partial is not None:
        in_specs.append(pl.BlockSpec(memory_space=pl.ANY))
        operands.append(partial)
        aliases = {6: 0}
    return pl.pallas_call(
        input_body,
        grid=(steps,),
        in_specs=in_specs,
        out_specs=by_row(512),
        out_shape=jax.ShapeDtypeStruct((total, 512), BF),
        scratch_shapes=[pltpu.VMEM((ROWS, 512), BF)],
        input_output_aliases=aliases,
        compiler_params=params(),
        cost_estimate=cost(4 * total * 512 * 1024 // parts, total * 4096 // parts),
        name="input_layer_%d" % part,
    )(*operands)


def between_cores(keep, send):
    return keep + swap(send, 0, 1).astype(F32)


def across_rep(total):
    got = [swap(total[k].astype(BF), k, 0) for k in (1, 2, 3)]
    return total[0], got


def along_z(total):
    got = [swap(total[j].astype(BF), 0, 2 * j) for j in (1, 2, 3)]
    return total[0], got


def gather_rep(piece):
    return [piece] + [swap(piece, k, 0) for k in (1, 2, 3)]


def add_up(kept, got):
    return kept + got[0].astype(F32) + got[1].astype(F32) + got[2].astype(F32)


def rebuild_body(where, *refs):
    ones, twos = refs[0:4], refs[4:8]
    conv, out, cond, bias, square, small = refs[8:]
    for k in range(4):
        quarter = where[1] ^ k
        row = pl.multiple_of(quarter * TILE, TILE)
        for t in range(2):
            for b in range(4):
                lane = (b & 1) * LANES + (b >> 1) * 512
                conv[t, pl.ds(row, TILE), pl.ds(lane, LANES)] = ones[k][
                    t * 64 + b * TILE : t * 64 + (b + 1) * TILE, :
                ]
                conv[t, pl.ds(row, TILE), pl.ds(lane + 256, LANES)] = twos[k][
                    t * 64 + b * TILE : t * 64 + (b + 1) * TILE, :
                ]
        for b in range(8):
            out[pl.ds(row, TILE), b * LANES : (b + 1) * LANES] = twos[k][
                128 + b * TILE : 128 + (b + 1) * TILE, :
            ]
        small[pl.ds(pl.multiple_of(quarter * 32, 32), 32), :] = twos[k][256:288, :]
    cond[...] = small[0:MEL, :]
    bias[...] = small[MEL : MEL + 2, :]
    total = (
        jnp.sum(conv[...] * conv[...])
        + jnp.sum(out[...] * out[...])
        + jnp.sum(cond[...] * cond[...])
        + jnp.sum(bias[...] * bias[...])
    )
    square[...] = jnp.full((8, LANES), total, F32)


def rebuild(where, ones, twos):
    spec = pl.BlockSpec(memory_space=pltpu.VMEM)
    return pl.pallas_call(
        rebuild_body,
        in_specs=[pl.BlockSpec(memory_space=pltpu.SMEM)] + [spec] * 8,
        out_specs=[spec] * 5,
        out_shape=[
            jax.ShapeDtypeStruct((2, 64, 1024), F32),
            jax.ShapeDtypeStruct((64, 1024), F32),
            jax.ShapeDtypeStruct((MEL, LANES), F32),
            jax.ShapeDtypeStruct((2, LANES), F32),
            jax.ShapeDtypeStruct((8, LANES), F32),
        ],
        scratch_shapes=[pltpu.VMEM((AUX, LANES), F32)],
        compiler_params=params(),
        name="rebuild",
    )(where, *ones, *twos)


def adamw_update(grad, moment, second, weight, factor, decay):
    clipped = grad * factor
    moment_new = beta_one * moment + (1.0 - beta_one) * clipped
    second_new = beta_two * second + (1.0 - beta_two) * clipped * clipped
    mean_hat = moment_new / (1.0 - beta_one**STEP)
    square_hat = second_new / (1.0 - beta_two**STEP)
    weight_new = weight - learn_rate * (
        mean_hat / (jnp.sqrt(square_hat) + epsilon) + decay * weight
    )
    return (moment_new, second_new, weight_new)


def local(
    inputs,
    mel_frames,
    utterance,
    keep_mask,
    res_grad,
    skip_grad,
    conv_weight,
    cond_weight,
    out_weight,
    biases,
    conv_first,
    conv_second,
    cond_first,
    cond_second,
    out_first,
    out_second,
    bias_first,
    bias_second,
):
    rows, width = inputs.shape
    span = DILATION_STEP
    split = lax.axis_size("rep") == 4 and lax.axis_size("seq") == 8
    seq, rep = lax.axis_index("seq"), lax.axis_index("rep")
    where = jnp.stack([seq % 2, rep, seq // 2]).astype(jnp.int32)

    conv_low = conv_weight.astype(BF).transpose(1, 0, 2)
    if split:
        w, o, bias_out = gather_quarters(
            where, conv_low, out_weight, cond_weight, biases.reshape(2, LANES)
        )
    else:
        w, o, bias_out = gather_plain(conv_low, out_weight, cond_weight, biases)

    tail = from_behind(inputs[rows - span :], BOTH, 1)
    prev_ids = from_behind(utterance[rows - span :], BOTH, 1)
    index = lax.axis_index(BOTH)
    shifted_ids = jnp.concatenate([prev_ids, utterance[: rows - span]], 0)
    linked = shifted_ids == utterance
    linked = linked & ((jnp.arange(rows) >= span) | (index > 0))
    aux = jnp.concatenate(
        [
            mel_frames,
            jnp.ones((1, rows), BF),
            keep_mask.astype(BF)[None],
            linked.astype(BF)[None],
            jnp.zeros((AUX - MEL - 3, rows), BF),
        ],
        0,
    )

    tile = 512
    if split:
        p_one, hid_one, keep_one, send_one, aux_one, sums = half_layer(
            0, split, tile, where, inputs, tail, aux, res_grad, skip_grad, w, o, ()
        )
        one = between_cores(keep_one, send_one)
        one = across_rep(one)
        p_two, hid_two, edge, keep_two, send_two = half_layer(
            1, split, tile, where, inputs, tail, aux, res_grad, skip_grad, w, o,
            (hid_one, p_one, w, aux_one, sums),
        )
    else:
        p_one, hid_one, grad_one, sums = half_layer(
            0, split, tile, where, inputs, tail, aux, res_grad, skip_grad, w, o, ()
        )
        p_two, hid_two, edge, grad_two, grad_out = half_layer(
            1, split, tile, where, inputs, tail, aux, res_grad, skip_grad, w, o,
            (hid_one, p_one, w),
        )

    returned = from_behind(edge[0], BOTH, -1)[None]
    if split:
        two = across_rep(between_cores(keep_two, send_two))
    input_part = input_layer(tile, 0, 2, res_grad, p_one, p_two, aux, w, edge, 1, None)
    if split:
        one = along_z(add_up(*one))
        two = along_z(add_up(*two))
    residual_out, skip_out = mixed_layer(tile, inputs, hid_one, hid_two, o, bias_out)
    if split:
        one = gather_rep(add_up(*one))
        two = gather_rep(add_up(*two))
    input_grad = input_layer(
        tile, 1, 2, res_grad, p_one, p_two, aux, w, returned, 0, input_part
    )

    if split:
        own_conv, own_out, own_cond, own_bias, square = rebuild(where, one, two)
        own_conv = own_conv.transpose(1, 0, 2)
        own_bias = own_bias.reshape(-1)
        parts = [[swap(square, 0, 2 * j + c) if j + c else square for c in (0, 1)] for j in range(4)]
        pairs = [(a + b)[0, 0] for a, b in parts]
        total = (pairs[0] + pairs[1]) + (pairs[2] + pairs[3])
    else:
        unmix = lambda g: mixed_columns(g)
        grad = unmix(jnp.concatenate([grad_one, grad_two], 1))
        grad_conv = jnp.stack([grad[0:512], grad[512:1024]], 1)
        grad_bias = jnp.concatenate([grad[1024 + ONES], sums[0]], 0)
        own = (
            lax.psum_scatter(grad_conv, "seq", scatter_dimension=0, tiled=True),
            lax.psum_scatter(grad[1024 : 1024 + MEL], "seq", scatter_dimension=1, tiled=True),
            lax.psum_scatter(grad_out, "seq", scatter_dimension=0, tiled=True),
            lax.psum_scatter(grad_bias, "seq", scatter_dimension=0, tiled=True),
        )
        own_conv, own_cond, own_out, own_bias = lax.psum(own, "rep")
        squares = (
            jnp.sum(own_conv * own_conv)
            + jnp.sum(own_cond * own_cond)
            + jnp.sum(own_out * own_out)
            + jnp.sum(own_bias * own_bias)
        )
        total = lax.psum(squares, "seq")

    grad_norm = jnp.sqrt(total)
    factor = clip_bound / jnp.maximum(grad_norm, clip_bound)
    conv_new = adamw_update(own_conv, conv_first, conv_second, conv_weight, factor, weight_decay)
    cond_new = adamw_update(own_cond, cond_first, cond_second, cond_weight, factor, weight_decay)
    out_new = adamw_update(own_out, out_first, out_second, out_weight, factor, weight_decay)
    bias_new = adamw_update(own_bias, bias_first, bias_second, biases, factor, 0.0)
    return (
        residual_out,
        skip_out,
        input_grad,
        grad_norm,
        *conv_new,
        *cond_new,
        *out_new,
        *bias_new,
    )


def solution(mesh):
    rows = P(BOTH, None)
    line = P(BOTH)
    conv = P("seq", None, None)
    cond = P(None, "seq")
    out = P("seq", None)
    bias = P("seq")
    placed = (
        rows,
        P(None, BOTH),
        line,
        line,
        rows,
        rows,
        conv,
        cond,
        out,
        bias,
        conv,
        conv,
        cond,
        cond,
        out,
        out,
        bias,
        bias,
    )
    return jax.shard_map(
        local,
        mesh=mesh,
        in_specs=placed,
        out_specs=(rows, rows, rows, P()) + (conv,) * 3 + (cond,) * 3 + (out,) * 3 + (bias,) * 3,
        check_vma=False,
    )
```

```python
import functools

import jax
import jax.numpy as jnp
from jax import lax
from jax.experimental import pallas as pl
from jax.experimental.pallas import tpu as pltpu
from jax.sharding import PartitionSpec as P

DILATION_STEP = 512
STEP = 10

beta_one = 0.9
beta_two = 0.999
learn_rate = 0.05
weight_decay = 0.01
epsilon = 1e-08
clip_bound = 1.0

LANES = 128
TILE = 16
AUX = 128
MEL = 80
ONES = 80
KEEP = 81
LINK = 82
ROWS = 512
BF = jnp.bfloat16
F32 = jnp.float32
BOTH = ("rep", "seq")


def from_behind(x, axis, by):
    count = lax.axis_size(axis)
    pairs = [(i, i + by) for i in range(count) if 0 <= i + by < count]
    return lax.ppermute(x, axis, pairs)


def swap(x, rep_bits, seq_bits):
    reps, seqs = lax.axis_size("rep"), lax.axis_size("seq")
    pairs = [
        (r * seqs + s, (r ^ rep_bits) * seqs + (s ^ seq_bits))
        for r in range(reps)
        for s in range(seqs)
    ]
    return lax.ppermute(x, BOTH, pairs)


def nt_dot(left, right):
    return lax.dot_general(
        left, right, (((1,), (1,)), ((), ())), preferred_element_type=F32
    )


def tn_dot(left, right):
    return lax.dot_general(
        left, right, (((0,), (0,)), ((), ())), preferred_element_type=F32
    )


def dot(left, right):
    return jnp.dot(left, right, preferred_element_type=F32)


def params(**more):
    return pltpu.CompilerParams(vmem_limit_bytes=58 * 2**20, **more)


def cost(flops, moved):
    return pl.CostEstimate(flops=int(flops), bytes_accessed=int(moved), transcendentals=0)


def whole(shape):
    return pl.BlockSpec(shape, lambda *_: (0,) * len(shape))


def spot():
    seq = lax.axis_index("seq")
    return seq % 2, lax.axis_index("rep"), seq // 2


VMEM = pl.BlockSpec(memory_space=pltpu.VMEM)
ANY = pl.BlockSpec(memory_space=pl.ANY)


OUT_PART = 8 * TILE
GATE_PART = 2 * 8 * TILE + 32
PART = GATE_PART + OUT_PART


def pack_body(conv, cond, bias, out, own, first, small):
    _, rep, _ = spot()
    small[0:MEL, :] = cond[...].astype(BF)
    small[MEL:96, :] = jnp.concatenate([bias[...], jnp.zeros((14, LANES), F32)], 0).astype(BF)
    small[96:AUX, :] = jnp.zeros((32, LANES), BF)
    for k in range(4):
        start = pl.multiple_of((rep ^ k) * TILE, TILE)
        for t in range(2):
            put_tiles(own.at[k], t * 128, conv[pl.ds(start, TILE), t, :])
        own[k, 256:GATE_PART, :] = small[pl.ds(2 * start, 32), :]
        put_tiles(own.at[k], GATE_PART, out[pl.ds(start, TILE), :])
    first[...] = own[0]


def pack_weights(conv, cond, bias, out):
    return pl.pallas_call(
        pack_body,
        in_specs=[VMEM] * 4,
        out_specs=[VMEM] * 2,
        out_shape=[
            jax.ShapeDtypeStruct((4, PART, LANES), BF),
            jax.ShapeDtypeStruct((PART, LANES), BF),
        ],
        scratch_shapes=[pltpu.VMEM((AUX, LANES), BF)],
        compiler_params=params(),
        name="pack_weights",
    )(conv, cond, bias, out)


def tail_body(x, _, tail):
    tail[...] = x[...]


def last_rows(x, after):
    return pl.pallas_call(
        tail_body,
        grid=(1,),
        in_specs=[pl.BlockSpec((ROWS, x.shape[1]), lambda i: (x.shape[0] // ROWS - 1, 0)), ANY],
        out_specs=whole((ROWS, x.shape[1])),
        out_shape=jax.ShapeDtypeStruct((ROWS, x.shape[1]), x.dtype),
        compiler_params=params(),
        name="last_rows",
    )(x, after)


def mixed_block(block):
    low, mid, top = block & 1, (block >> 1) & 1, (block >> 2) & 1
    return low + 4 * mid + 2 * top


def each_part(own, stack, sides, write):
    core, rep, z = spot()
    for c in range(2):
        for j in range(4):
            for k in range(4):
                if j == 0:
                    source = own[c].at[k]
                elif k == 0:
                    source = stack[c].at[pl.ds((j - 1) * PART, PART), :]
                else:
                    source = sides[c][k - 1].at[pl.ds((j - 1) * PART, PART), :]
                write(source, 2 * (z ^ j) + (core ^ c), rep ^ k)


def unpack(refs, w, o, bias_out, small):
    def write(source, shard, quarter):
        row = pl.multiple_of(64 * shard + TILE * quarter, TILE)
        for b in range(8):
            lanes = pl.ds(mixed_block(b) * LANES, LANES)
            w[pl.ds(row, TILE), lanes] = source[b * TILE : (b + 1) * TILE, :]
            w[pl.ds(512 + row, TILE), lanes] = source[128 + b * TILE : 128 + (b + 1) * TILE, :]
        small[shard, pl.ds(pl.multiple_of(32 * quarter, 32), 32), :] = source[256:GATE_PART, :]
        for b in range(8):
            base = GATE_PART + b * TILE
            o[pl.ds(row, TILE), b * LANES : (b + 1) * LANES] = source[base : base + TILE, :]

    each_part(refs[0:2], refs[2:4], (refs[4:7], refs[7:10]), write)
    blank = jnp.zeros((TILE - 1, LANES), BF)
    for s in range(8):
        lane = mixed_block(s) * LANES
        w[1024 : 1024 + MEL, lane : lane + LANES] = small[s, 0:MEL, :]
        tail = small[s, MEL : MEL + TILE, :]
        for e in range(2):
            if s < 4:
                at = mixed_block(2 * s + e) * LANES
                w[1104:1120, at : at + LANES] = jnp.concatenate([tail[e : e + 1], blank], 0)
            else:
                at = (2 * (s - 4) + e) * LANES
                bias_out[:, at : at + LANES] = jnp.broadcast_to(tail[e : e + 1].astype(F32), (8, LANES))
    w[1120:1152, :] = jnp.zeros((32, w.shape[1]), BF)


def across_hops(own, stack):
    across = [swap(stack, k, 0) for k in (1, 2, 3)]
    return [own, swap(own, 0, 1), stack, swap(stack, 0, 1), *across, *[swap(a, 0, 1) for a in across]]


def mixed_columns(x):
    rows, columns = x.shape
    return x.reshape(rows, 2, 2, columns // 4).transpose(0, 2, 1, 3).reshape(rows, columns)


def gather_plain(conv_weight, out_weight, cond_weight, biases):
    conv = conv_weight.astype(BF).transpose(1, 0, 2)
    conv_all = lax.all_gather(conv, "seq", axis=1, tiled=True)
    cond_all = lax.all_gather(cond_weight.astype(BF), "seq", axis=1, tiled=True)
    out_all = lax.all_gather(out_weight.astype(BF), "seq", axis=0, tiled=True)
    bias_all = lax.all_gather(biases.astype(BF), "seq", axis=0, tiled=True)
    gates = cond_all.shape[1]
    w = jnp.concatenate(
        [
            conv_all[0],
            conv_all[1],
            cond_all,
            bias_all[None, :gates],
            jnp.zeros((AUX - MEL - 1, gates), BF),
        ],
        0,
    )
    bias_out = jnp.broadcast_to(bias_all[None, gates:].astype(F32), (8, gates))
    return mixed_columns(w), out_all, bias_out


def sums_body(res, skp, *refs):
    sums = refs[-1]

    @pl.when(pl.program_id(0) == 0)
    def _():
        sums[...] = jnp.zeros_like(sums)

    for n, part in enumerate((res, skp)):
        total = jnp.sum(part[...].astype(F32), 0, keepdims=True)
        sums[:, n * 512 : (n + 1) * 512] += jnp.broadcast_to(total, (8, 512))


def sum_columns(rows, res, skp, after):
    total = res.shape[0]
    by_row = pl.BlockSpec((rows, 512), lambda i: (i, 0))
    return pl.pallas_call(
        sums_body,
        grid=(total // rows,),
        in_specs=[by_row, by_row] + [ANY] * len(after),
        out_specs=whole((8, 1024)),
        out_shape=jax.ShapeDtypeStruct((8, 1024), F32),
        compiler_params=params(),
        cost_estimate=cost(total * 1024, total * 2048),
        name="sum_columns",
    )(res, skp, *after)


def emit_pieces(outs, write):
    core, rep, z = spot()
    for c, dest in enumerate(outs):

        def one(n, carry, c=c, dest=dest):
            k, j = n // 4, n % 4
            write(dest.at[k, j], 2 * (z ^ j) + (core ^ c), rep ^ k)
            return carry

        lax.fori_loop(0, 16, one, 0)


def put_tiles(dest, base, value, order=lambda b: b):
    value = value.astype(dest.dtype)
    for b in range(value.shape[1] // LANES):
        lane = order(b) * LANES
        dest[base + b * TILE : base + (b + 1) * TILE, :] = value[:, lane : lane + LANES]


def gates_body(split, subs, x, tail, mel, keep, ids, tail_ids, res, skp, *refs):
    if split:
        sums, parts, refs = refs[0], refs[1:11], refs[11:]
        p, hid, flags, edge, w, o, bias_out, keep_out, send_out = refs[:9]
        xe, carry, carry_ids, acc, acc_out, small, small_low = refs[9:]
    else:
        w, o, p, hid, flags, edge, grad, grad_out, xe, carry, carry_ids, acc, acc_out = refs
    step, last = pl.program_id(0), pl.num_programs(0) - 1
    rows, half = x.shape[0], p.shape[1] // 4

    @pl.when(step == 0)
    def _():
        carry[...] = tail[...]
        carry_ids[...] = jnp.where(lax.axis_index(BOTH) > 0, tail_ids[...], -1)
        acc[...] = jnp.zeros_like(acc)
        acc_out[...] = jnp.zeros_like(acc_out)
        if split:
            unpack(parts, w, o, bias_out, small_low)

    ids_now = ids[...]
    ids_past = carry_ids[...]
    if rows > ROWS:
        ids_past = jnp.concatenate([ids_past, ids_now[:, 0 : rows - ROWS]], 1)
    place = lax.broadcasted_iota(jnp.int32, (TILE, rows), 0)
    mark = jnp.where(
        place == 0,
        1.0,
        jnp.where(
            place == KEEP - ONES,
            keep[...].astype(F32),
            jnp.where(place == LINK - ONES, (ids_now == ids_past).astype(F32), 0.0),
        ),
    ).astype(BF)
    flags[...] = mark
    side = jnp.concatenate([mel[...], mark, jnp.zeros((32, rows), BF)], 0).T
    link = side[:, LINK : LINK + 1]
    kept_rows = side[:, KEEP : KEEP + 1].astype(F32)
    xe[:, 0:512] = x[...]
    xe[0:ROWS, 512:1024] = carry[...] * link[0:ROWS]
    if rows > ROWS:
        xe[ROWS:, 512:1024] = x[0 : rows - ROWS, :] * link[ROWS:]
    xe[:, 1024:1152] = side
    carry[...] = x[rows - ROWS :, :]
    carry_ids[...] = ids_now[:, rows - ROWS :]

    size = rows // subs
    for s in range(subs):
        at = slice(s * size, (s + 1) * size)
        up_all = nt_dot(res[at, :], o[:, 0:512]) + nt_dot(skp[at, :], o[:, 512:1024])
        for n in range(2):
            base = n * 2 * half
            pre = dot(xe[at, :], w[:, base : base + 2 * half])
            up = up_all[:, n * half : (n + 1) * half]
            filt = jnp.tanh(pre[:, :half])
            gate = 0.5 * jnp.tanh(0.5 * pre[:, half:]) + 0.5
            kept = kept_rows[at] * gate
            hidden = filt * kept
            hid[at, n * half : (n + 1) * half] = hidden.astype(BF)
            p[at, base : base + half] = (up * kept * (1.0 - filt * filt)).astype(BF)
            p[at, base + half : base + 2 * half] = (up * hidden * (1.0 - gate)).astype(BF)
    acc[...] += tn_dot(xe[...], p[...])
    acc_out[:, 0:512] += tn_dot(hid[...], res[...])
    acc_out[:, 512:1024] += tn_dot(hid[...], skp[...])

    @pl.when(step == 0)
    def _():
        past = nt_dot(p[0:ROWS, :], w[512:1024, :])
        edge[...] = (past * link[0:ROWS].astype(F32)).astype(BF)

    @pl.when(step == last)
    def _():
        if not split:
            grad[...] = acc[...]
            grad_out[...] = acc_out[...]
            return
        small[...] = jnp.zeros_like(small)
        for s in range(8):
            lane = mixed_block(s) * LANES
            small[s, 0:MEL, :] = acc[1024 : 1024 + MEL, lane : lane + LANES]
            for e in range(2):
                if s < 4:
                    lane = mixed_block(2 * s + e) * LANES
                    line = acc[1024 + ONES : 1024 + ONES + 1, lane : lane + LANES]
                else:
                    lane = (2 * (s - 4) + e) * LANES
                    line = sums[0:1, lane : lane + LANES]
                small[s, MEL + e : MEL + e + 1, :] = line

        def write(dest, shard, quarter):
            row = pl.multiple_of(64 * shard + TILE * quarter, TILE)
            put_tiles(dest, 0, acc[pl.ds(row, TILE), :], mixed_block)
            put_tiles(dest, 128, acc[pl.ds(512 + row, TILE), :], mixed_block)
            at = pl.multiple_of(32 * quarter, 32)
            dest[256:GATE_PART, :] = small[shard, pl.ds(at, 32), :].astype(dest.dtype)
            put_tiles(dest, GATE_PART, acc_out[pl.ds(row, TILE), :])

        emit_pieces((keep_out, send_out), write)


def gates_layer(split, rows, subs, x, tail, mel, keep, ids, tail_ids, res, skp, extra):
    total = x.shape[0]
    steps = total // rows
    by_row = lambda columns: pl.BlockSpec((rows, columns), lambda i: (i, 0))
    by_lane = lambda high: pl.BlockSpec((high, rows), lambda i: (0, i))
    in_specs = [
        by_row(512),
        whole((ROWS, 512)),
        by_lane(MEL),
        by_lane(1),
        by_lane(1),
        whole((1, ROWS)),
        by_row(512),
        by_row(512),
    ] + [whole(e.shape) for e in extra]
    out_specs = [
        by_row(1024),
        by_row(512),
        by_lane(TILE),
        whole((ROWS, 512)),
    ]
    out_shape = [
        jax.ShapeDtypeStruct((total, 1024), BF),
        jax.ShapeDtypeStruct((total, 512), BF),
        jax.ShapeDtypeStruct((TILE, total), BF),
        jax.ShapeDtypeStruct((ROWS, 512), BF),
    ]
    if split:
        more = [
            ((1024 + AUX, 1024), BF),
            ((512, 1024), BF),
            ((8, 1024), F32),
            ((4, 4, PART, LANES), BF),
            ((4, 4, PART, LANES), BF),
        ]
    else:
        more = [((1024 + AUX, 1024), F32), ((512, 1024), F32)]
    for shape, dtype in more:
        out_specs.append(whole(shape))
        out_shape.append(jax.ShapeDtypeStruct(shape, dtype))
    scratch = [
        pltpu.VMEM((rows, 1024 + AUX), BF),
        pltpu.VMEM((ROWS, 512), BF),
        pltpu.VMEM((1, ROWS), jnp.int32),
        pltpu.VMEM((1024 + AUX, 1024), F32),
        pltpu.VMEM((512, 1024), F32),
    ]
    if split:
        scratch += [pltpu.VMEM((8, AUX, LANES), F32), pltpu.VMEM((8, AUX, LANES), BF)]
    return pl.pallas_call(
        functools.partial(gates_body, split, subs),
        grid=(steps,),
        in_specs=in_specs,
        out_specs=out_specs,
        out_shape=out_shape,
        scratch_shapes=scratch,
        compiler_params=params(),
        cost_estimate=cost(6.75 * 2 * total * 512 * 1024, total * 8000),
        name="gates_layer",
    )(x, tail, mel, keep, ids, tail_ids, res, skp, *extra)


def mixed_body(x, hid, o, bias, rest, edge, *refs):
    residual, skip, patch = refs[-3:]
    mixed = dot(hid[...], o[...]) + bias[0:1, :]
    residual[...] = (x[...].astype(F32) + mixed[:, 0:512]).astype(BF)
    skip[...] = mixed[:, 512:1024].astype(BF)

    @pl.when(pl.program_id(0) == 0)
    def _():
        patch[...] = (rest[...] + edge[...].astype(F32)).astype(BF)


def mixed_layer(rows, x, hid, o, bias, rest, edge, input_grad, after):
    total = x.shape[0]
    by_row = pl.BlockSpec((rows, 512), lambda i: (i, 0))
    last = pl.BlockSpec((ROWS, 512), lambda i: (total // ROWS - 1, 0))
    operands = (x, hid, o, bias, rest, edge, input_grad, *after)
    return pl.pallas_call(
        mixed_body,
        grid=(total // rows,),
        in_specs=[by_row, by_row, whole((512, 1024)), whole((8, 1024)), whole((ROWS, 512)), whole((ROWS, 512))]
        + [ANY] * (1 + len(after)),
        out_specs=[by_row, by_row, last],
        out_shape=[jax.ShapeDtypeStruct((total, 512), BF)] * 3,
        input_output_aliases={6: 2},
        compiler_params=params(),
        cost_estimate=cost(2 * total * 512 * 1024, total * 4096),
        name="mixed_layer",
    )(*operands)


def input_body(res, p, flags, w, *refs):
    out, rest, carry = refs[-3:]
    step = pl.program_id(0)
    rows = res.shape[0]
    link = flags[...].T[:, LINK - MEL : LINK - MEL + 1].astype(F32)
    both = nt_dot(p[...], w[...])
    past = both[:, 512:1024] * link
    now = res[...].astype(F32) + both[:, 0:512]

    @pl.when(step == 0)
    def _():
        rest[...] = now[rows - ROWS :]
        carry[...] = jnp.zeros_like(carry)

    if rows > ROWS:
        out[0 : rows - ROWS, :] = (now[0 : rows - ROWS] + past[ROWS:]).astype(BF)
    out[rows - ROWS :, :] = (now[rows - ROWS :] + carry[...]).astype(BF)
    carry[...] = past[0:ROWS]


def input_layer(rows, res, p, flags, w, after):
    total = res.shape[0]
    steps = total // rows
    by_row = lambda columns: pl.BlockSpec((rows, columns), lambda i: (steps - 1 - i, 0))
    return pl.pallas_call(
        input_body,
        grid=(steps,),
        in_specs=[
            by_row(512),
            by_row(1024),
            pl.BlockSpec((TILE, rows), lambda i: (0, steps - 1 - i)),
            pl.BlockSpec((1024, 1024), lambda i: (0, 0)),
        ]
        + [ANY] * len(after),
        out_specs=[by_row(512), whole((ROWS, 512))],
        out_shape=[
            jax.ShapeDtypeStruct((total, 512), BF),
            jax.ShapeDtypeStruct((ROWS, 512), F32),
        ],
        scratch_shapes=[pltpu.VMEM((ROWS, 512), F32)],
        compiler_params=params(),
        cost_estimate=cost(4 * total * 512 * 1024, total * 4096),
        name="input_layer",
    )(res, p, flags, w, *after)


def cores_body(keep, got, edge, *outs):
    for n in range(4):
        outs[n][...] = (keep[n].astype(F32) + got[n].astype(F32)).astype(outs[n].dtype)
    outs[4][...] = edge[...]


def add_cores(keep, got, edge):
    spec = pl.BlockSpec((4, 1, PART, LANES), lambda i: (0, i, 0, 0))
    part = pl.BlockSpec((ROWS // 4, 512), lambda i: (i, 0))
    return pl.pallas_call(
        cores_body,
        grid=(4,),
        in_specs=[spec, spec, part],
        out_specs=[pl.BlockSpec((1, PART, LANES), lambda i: (i, 0, 0))] * 4 + [part],
        out_shape=[jax.ShapeDtypeStruct((4, PART, LANES), BF if n else F32) for n in range(4)]
        + [jax.ShapeDtypeStruct(edge.shape, BF)],
        compiler_params=params(),
        cost_estimate=cost(10**6, 8 * 10**6),
        name="add_cores",
    )(keep, got, edge)


def hop_body(keep, g1, g2, g3, *refs):
    outs = refs[-4:]
    for n in range(4):
        total = keep[n] + g1[n].astype(F32) + g2[n].astype(F32) + g3[n].astype(F32)
        outs[n][...] = total.astype(outs[n].dtype)


def add_hop(parts, after):
    return pl.pallas_call(
        hop_body,
        in_specs=[VMEM] * 4 + [ANY] * len(after),
        out_specs=[VMEM] * 4,
        out_shape=[jax.ShapeDtypeStruct((PART, LANES), BF if n else F32) for n in range(4)],
        compiler_params=params(),
        cost_estimate=cost(10**6, 3 * 10**6),
        name="add_hop",
    )(*parts, *after)


def last_body(keep, g1, g2, g3, *refs):
    total, square = refs[-2:]
    total[...] = keep[...] + g1[...].astype(F32) + g2[...].astype(F32) + g3[...].astype(F32)
    square[...] = jnp.full(square.shape, jnp.sum(total[...] * total[...]), F32)


def add_last(parts, devices, after):
    return pl.pallas_call(
        last_body,
        in_specs=[VMEM] * 4 + [ANY] * len(after),
        out_specs=[VMEM] * 2,
        out_shape=[
            jax.ShapeDtypeStruct((PART, LANES), F32),
            jax.ShapeDtypeStruct((devices, LANES), F32),
        ],
        compiler_params=params(),
        cost_estimate=cost(10**6, 10**6),
        name="add_last",
    )(*parts, *after)


def adamw_update(grad, moment, second, weight, factor, decay):
    clipped = grad * factor
    moment_new = beta_one * moment + (1.0 - beta_one) * clipped
    second_new = beta_two * second + (1.0 - beta_two) * clipped * clipped
    mean_hat = moment_new / (1.0 - beta_one**STEP)
    square_hat = second_new / (1.0 - beta_two**STEP)
    weight_new = weight - learn_rate * (
        mean_hat / (jnp.sqrt(square_hat) + epsilon) + decay * weight
    )
    return (moment_new, second_new, weight_new)


def update_body(*refs):
    squares, parts = refs[0], refs[1:5]
    conv, cond, out, bias = refs[5:8], refs[8:11], refs[11:14], refs[14:17]
    norm, new, small = refs[17], refs[18:30], refs[30]
    _, rep, _ = spot()
    grad_norm = jnp.sqrt(jnp.sum(squares[...], 0, keepdims=True))
    norm[...] = grad_norm
    factor = clip_bound / jnp.maximum(grad_norm, clip_bound)

    def step(grad, old, dest, at, decay):
        got = adamw_update(grad, *[ref[at] for ref in old], factor, decay)
        for ref, value in zip(dest, got):
            ref[at] = value

    for k in range(4):
        row = pl.multiple_of((rep ^ k) * TILE, TILE)
        for b in range(8):
            lanes = slice(b * LANES, (b + 1) * LANES)
            for t in range(2):
                base = t * 128 + b * TILE
                step(parts[k][base : base + TILE, :], conv, new[0:3], (pl.ds(row, TILE), t, lanes), weight_decay)
            base = GATE_PART + b * TILE
            step(parts[k][base : base + TILE, :], out, new[6:9], (pl.ds(row, TILE), lanes), weight_decay)
        small[pl.ds(2 * row, 32), :] = parts[k][256:GATE_PART, :]
    step(small[0:MEL, :], cond, new[3:6], (slice(0, MEL), slice(0, LANES)), weight_decay)
    step(small[MEL : MEL + 2, :], bias, new[9:12], (slice(0, 2), slice(0, LANES)), 0.0)


def update(squares, parts, conv, cond, out, bias):
    shapes = [(1, LANES)]
    for group in (conv, cond, out, bias):
        shapes += [group[0].shape] * 3
    return pl.pallas_call(
        update_body,
        in_specs=[VMEM] * 17,
        out_specs=[VMEM] * 13,
        out_shape=[jax.ShapeDtypeStruct(s, F32) for s in shapes],
        scratch_shapes=[pltpu.VMEM((AUX, LANES), F32)],
        compiler_params=params(),
        name="update",
    )(squares, *parts, *conv, *cond, *out, *bias)


def local(
    inputs,
    mel_frames,
    utterance,
    keep_mask,
    res_grad,
    skip_grad,
    conv_weight,
    cond_weight,
    out_weight,
    biases,
    conv_first,
    conv_second,
    cond_first,
    cond_second,
    out_first,
    out_second,
    bias_first,
    bias_second,
):
    rows, width = inputs.shape
    span = DILATION_STEP
    split = lax.axis_size("rep") == 4 and lax.axis_size("seq") == 8
    tile = 1024

    if split:
        own, first = pack_weights(conv_weight, cond_weight, biases.reshape(2, LANES), out_weight)
        stack = jnp.concatenate([swap(first, 0, 2 * j) for j in (1, 2, 3)], 0)
        parts = across_hops(own, stack)
        sums = sum_columns(2 * tile, res_grad, skip_grad, (stack,))
        last = last_rows(inputs, stack)
    else:
        w, o, bias_out = gather_plain(conv_weight, out_weight, cond_weight, biases)
        sums = sum_columns(2 * tile, res_grad, skip_grad, ())
        last = inputs[rows - span :]

    tail = from_behind(last, BOTH, 1)
    tail_ids = from_behind(utterance[rows - span :], BOTH, 1)
    samples = (
        inputs,
        tail,
        mel_frames,
        keep_mask.reshape(1, rows),
        utterance.reshape(1, rows),
        tail_ids.reshape(1, span),
        res_grad,
        skip_grad,
    )
    if split:
        p, hid, flags, edge, w, o, bias_out, keep, send = gates_layer(split, tile, 2, *samples, (sums, *parts))
        got = add_cores(keep, swap(send, 0, 1), edge)
        edge = got[4]
        part = [got[0]] + [swap(got[n], n, 0) for n in (1, 2, 3)]
        after = (got[1],)
    else:
        p, hid, flags, edge, grad, grad_out = gates_layer(split, tile, 2, *samples, (w, o))
        after = ()

    returned = from_behind(edge, BOTH, -1)
    input_grad, rest = input_layer(tile, res_grad, p, flags, w, after)
    if split:
        got = add_hop(part, (rest,))
        part = [got[0]] + [swap(got[n], 0, 2 * n) for n in (1, 2, 3)]
        after = (got[1],)
    residual_out, skip_out, input_grad = mixed_layer(
        tile, inputs, hid, o, bias_out, rest, returned, input_grad, after
    )

    if split:
        total, square = add_last(part, lax.axis_size(BOTH), (skip_out,))
        part = [total] + [swap(total, n, 0) for n in (1, 2, 3)]
        squares = lax.all_to_all(square, BOTH, 0, 0, tiled=True)
        fold = lambda v: v.reshape(2, LANES)
        norm, *new = update(
            squares,
            part,
            (conv_first, conv_second, conv_weight),
            (cond_first, cond_second, cond_weight),
            (out_first, out_second, out_weight),
            (fold(bias_first), fold(bias_second), fold(biases)),
        )
        grad_norm = norm[0, 0]
        new = new[:9] + [v.reshape(-1) for v in new[9:]]
    else:
        grad = mixed_columns(grad)
        grad_conv = jnp.stack([grad[0:512], grad[512:1024]], 1)
        grad_bias = jnp.concatenate([grad[1024 + ONES], sums[0]], 0)
        own = (
            lax.psum_scatter(grad_conv, "seq", scatter_dimension=0, tiled=True),
            lax.psum_scatter(grad[1024 : 1024 + MEL], "seq", scatter_dimension=1, tiled=True),
            lax.psum_scatter(grad_out, "seq", scatter_dimension=0, tiled=True),
            lax.psum_scatter(grad_bias, "seq", scatter_dimension=0, tiled=True),
        )
        own = lax.psum(own, "rep")
        grad_norm = jnp.sqrt(lax.psum(sum(jnp.sum(g * g) for g in own), "seq"))
        factor = clip_bound / jnp.maximum(grad_norm, clip_bound)
        new = [
            *adamw_update(own[0], conv_first, conv_second, conv_weight, factor, weight_decay),
            *adamw_update(own[1], cond_first, cond_second, cond_weight, factor, weight_decay),
            *adamw_update(own[2], out_first, out_second, out_weight, factor, weight_decay),
            *adamw_update(own[3], bias_first, bias_second, biases, factor, 0.0),
        ]
    return (residual_out, skip_out, input_grad, grad_norm, *new)


def solution(mesh):
    rows = P(BOTH, None)
    line = P(BOTH)
    conv = P("seq", None, None)
    cond = P(None, "seq")
    out = P("seq", None)
    bias = P("seq")
    placed = (
        rows,
        P(None, BOTH),
        line,
        line,
        rows,
        rows,
        conv,
        cond,
        out,
        bias,
        conv,
        conv,
        cond,
        cond,
        out,
        out,
        bias,
        bias,
    )
    return jax.shard_map(
        local,
        mesh=mesh,
        in_specs=placed,
        out_specs=(rows, rows, rows, P()) + (conv,) * 3 + (cond,) * 3 + (out,) * 3 + (bias,) * 3,
        check_vma=False,
    )
```

```python
import functools

import jax
import jax.numpy as jnp
from jax import lax
from jax.experimental import pallas as pl
from jax.experimental.pallas import tpu as pltpu
from jax.sharding import PartitionSpec as P

DILATION_STEP = 512
STEP = 10

beta_one = 0.9
beta_two = 0.999
learn_rate = 0.05
weight_decay = 0.01
epsilon = 1e-08
clip_bound = 1.0

LANES = 128
TILE = 16
AUX = 128
MEL = 80
ONES = 80
KEEP = 81
LINK = 82
ROWS = 512
GATES_MIB = 52
ARRIVE = 10**10
BF = jnp.bfloat16
F32 = jnp.float32
BOTH = ("rep", "seq")


def from_behind(x, axis, by):
    count = lax.axis_size(axis)
    pairs = [(i, i + by) for i in range(count) if 0 <= i + by < count]
    return lax.ppermute(x, axis, pairs)


def swap(x, rep_bits, seq_bits):
    reps, seqs = lax.axis_size("rep"), lax.axis_size("seq")
    pairs = [
        (r * seqs + s, (r ^ rep_bits) * seqs + (s ^ seq_bits))
        for r in range(reps)
        for s in range(seqs)
    ]
    return lax.ppermute(x, BOTH, pairs)


def nt_dot(left, right):
    return lax.dot_general(
        left, right, (((1,), (1,)), ((), ())), preferred_element_type=F32
    )


def tn_dot(left, right):
    return lax.dot_general(
        left, right, (((0,), (0,)), ((), ())), preferred_element_type=F32
    )


def dot(left, right):
    return jnp.dot(left, right, preferred_element_type=F32)


TOKEN = jax.ShapeDtypeStruct((8, LANES), F32)


def params(mib=24):
    return pltpu.CompilerParams(vmem_limit_bytes=mib * 2**20)


def cost(flops, moved):
    return pl.CostEstimate(flops=int(flops), bytes_accessed=int(moved), transcendentals=0)


def whole(shape):
    return pl.BlockSpec(shape, lambda *_: (0,) * len(shape))


def spot():
    seq = lax.axis_index("seq")
    return seq % 2, lax.axis_index("rep"), seq // 2


VMEM = pl.BlockSpec(memory_space=pltpu.VMEM)
ANY = pl.BlockSpec(memory_space=pl.ANY)


OUT_PART = 8 * TILE
GATE_PART = 2 * 8 * TILE + 32
PART = GATE_PART + OUT_PART


def pack_body(conv, cond, bias, out, own, first, small):
    _, rep, _ = spot()
    small[0:MEL, :] = cond[...].astype(BF)
    small[MEL:96, :] = jnp.concatenate([bias[...], jnp.zeros((14, LANES), F32)], 0).astype(BF)
    small[96:AUX, :] = jnp.zeros((32, LANES), BF)
    for k in range(4):
        start = pl.multiple_of((rep ^ k) * TILE, TILE)
        for t in range(2):
            put_tiles(own.at[k], t * 128, conv[pl.ds(start, TILE), t, :])
        own[k, 256:GATE_PART, :] = small[pl.ds(2 * start, 32), :]
        put_tiles(own.at[k], GATE_PART, out[pl.ds(start, TILE), :])
    first[...] = own[0]


def pack_weights(conv, cond, bias, out):
    return pl.pallas_call(
        pack_body,
        in_specs=[VMEM] * 4,
        out_specs=[VMEM] * 2,
        out_shape=[
            jax.ShapeDtypeStruct((4, PART, LANES), BF),
            jax.ShapeDtypeStruct((PART, LANES), BF),
        ],
        scratch_shapes=[pltpu.VMEM((AUX, LANES), BF)],
        compiler_params=params(58),
        name="pack_weights",
    )(conv, cond, bias, out)


def tail_body(x, _, tail):
    tail[...] = x[...]


def last_rows(x, after):
    return pl.pallas_call(
        tail_body,
        grid=(1,),
        in_specs=[pl.BlockSpec((ROWS, x.shape[1]), lambda i: (x.shape[0] // ROWS - 1, 0)), ANY],
        out_specs=whole((ROWS, x.shape[1])),
        out_shape=jax.ShapeDtypeStruct((ROWS, x.shape[1]), x.dtype),
        compiler_params=params(63),
        name="last_rows",
    )(x, after)


def arrive_body(_, token):
    token[...] = jnp.zeros_like(token)


def arrived_by(array):
    return pl.pallas_call(
        arrive_body,
        in_specs=[ANY],
        out_specs=VMEM,
        out_shape=TOKEN,
        compiler_params=params(63),
        cost_estimate=cost(ARRIVE, 4096),
        name="arrived_by",
    )(array)


def mixed_block(block):
    low, mid, top = block & 1, (block >> 1) & 1, (block >> 2) & 1
    return low + 4 * mid + 2 * top


def each_part(own, stack, sides, write):
    core, rep, z = spot()
    for c in range(2):
        for j in range(4):
            for k in range(4):
                if j == 0:
                    source = own[c].at[k]
                elif k == 0:
                    source = stack[c].at[pl.ds((j - 1) * PART, PART), :]
                else:
                    source = sides[c][k - 1].at[pl.ds((j - 1) * PART, PART), :]
                write(source, 2 * (z ^ j) + (core ^ c), rep ^ k)


def unpack(refs, w, o, bias_out, small):
    def write(source, shard, quarter):
        row = pl.multiple_of(64 * shard + TILE * quarter, TILE)
        for b in range(8):
            lanes = pl.ds(mixed_block(b) * LANES, LANES)
            w[pl.ds(row, TILE), lanes] = source[b * TILE : (b + 1) * TILE, :]
            w[pl.ds(512 + row, TILE), lanes] = source[128 + b * TILE : 128 + (b + 1) * TILE, :]
        small[shard, pl.ds(pl.multiple_of(32 * quarter, 32), 32), :] = source[256:GATE_PART, :]
        for b in range(8):
            base = GATE_PART + b * TILE
            o[pl.ds(row, TILE), b * LANES : (b + 1) * LANES] = source[base : base + TILE, :]

    each_part(refs[0:2], refs[2:4], (refs[4:7], refs[7:10]), write)
    blank = jnp.zeros((TILE - 1, LANES), BF)
    for s in range(8):
        lane = mixed_block(s) * LANES
        w[1024 : 1024 + MEL, lane : lane + LANES] = small[s, 0:MEL, :]
        tail = small[s, MEL : MEL + TILE, :]
        for e in range(2):
            if s < 4:
                at = mixed_block(2 * s + e) * LANES
                w[1104:1120, at : at + LANES] = jnp.concatenate([tail[e : e + 1], blank], 0)
            else:
                at = (2 * (s - 4) + e) * LANES
                bias_out[:, at : at + LANES] = jnp.broadcast_to(tail[e : e + 1].astype(F32), (8, LANES))
    w[1120:1152, :] = jnp.zeros((32, w.shape[1]), BF)


def across_hops(own, stack):
    across = [swap(stack, k, 0) for k in (1, 2, 3)]
    return [own, swap(own, 0, 1), stack, swap(stack, 0, 1), *across, *[swap(a, 0, 1) for a in across]]


def mixed_columns(x):
    rows, columns = x.shape
    return x.reshape(rows, 2, 2, columns // 4).transpose(0, 2, 1, 3).reshape(rows, columns)


def gather_plain(conv_weight, out_weight, cond_weight, biases):
    conv = conv_weight.astype(BF).transpose(1, 0, 2)
    conv_all = lax.all_gather(conv, "seq", axis=1, tiled=True)
    cond_all = lax.all_gather(cond_weight.astype(BF), "seq", axis=1, tiled=True)
    out_all = lax.all_gather(out_weight.astype(BF), "seq", axis=0, tiled=True)
    bias_all = lax.all_gather(biases.astype(BF), "seq", axis=0, tiled=True)
    gates = cond_all.shape[1]
    w = jnp.concatenate(
        [
            conv_all[0],
            conv_all[1],
            cond_all,
            bias_all[None, :gates],
            jnp.zeros((AUX - MEL - 1, gates), BF),
        ],
        0,
    )
    bias_out = jnp.broadcast_to(bias_all[None, gates:].astype(F32), (8, gates))
    return mixed_columns(w), out_all, bias_out


def emit_pieces(outs, write):
    core, rep, z = spot()
    for c, dest in enumerate(outs):

        def one(n, carry, c=c, dest=dest):
            k, j = n // 4, n % 4
            write(dest.at[k, j], 2 * (z ^ j) + (core ^ c), rep ^ k)
            return carry

        lax.fori_loop(0, 16, one, 0)


def put_tiles(dest, base, value, order=lambda b: b):
    value = value.astype(dest.dtype)
    for b in range(value.shape[1] // LANES):
        lane = order(b) * LANES
        dest[base + b * TILE : base + (b + 1) * TILE, :] = value[:, lane : lane + LANES]


def gates_body(split, subs, x, tail, mel, keep, ids, tail_ids, res, skp, *refs):
    if split:
        parts, refs = refs[0:10], refs[11:]
        p, hid, flags, edge, w, o, bias_out, keep_out, send_out = refs[:9]
        xe, carry, carry_ids, acc, acc_out, sums, small, small_low, arrived, *held = refs[9:]
    else:
        w, o, p, hid, flags, edge, grad, grad_out, sums, xe, carry, carry_ids, acc, acc_out = refs
    step, last = pl.program_id(0), pl.num_programs(0) - 1
    rows, half = x.shape[0], p.shape[1] // 4

    @pl.when(step == 0)
    def _():
        carry[...] = tail[...]
        carry_ids[...] = jnp.where(lax.axis_index(BOTH) > 0, tail_ids[...], -1)
        acc[...] = jnp.zeros_like(acc)
        acc_out[...] = jnp.zeros_like(acc_out)
        sums[...] = jnp.zeros_like(sums)
        if split:
            copies = [
                pltpu.make_async_copy(part, here, arrived.at[n])
                for n, (part, here) in enumerate(zip(parts, held))
            ]
            for copy in copies:
                copy.start()
            for copy in copies:
                copy.wait()
            unpack(held, w, o, bias_out, small_low)

    ids_now = ids[...]
    ids_past = carry_ids[...]
    if rows > ROWS:
        ids_past = jnp.concatenate([ids_past, ids_now[:, 0 : rows - ROWS]], 1)
    place = lax.broadcasted_iota(jnp.int32, (TILE, rows), 0)
    mark = jnp.where(
        place == 0,
        1.0,
        jnp.where(
            place == KEEP - ONES,
            keep[...].astype(F32),
            jnp.where(place == LINK - ONES, (ids_now == ids_past).astype(F32), 0.0),
        ),
    ).astype(BF)
    flags[...] = mark
    side = jnp.concatenate([mel[...], mark, jnp.zeros((32, rows), BF)], 0).T
    link = side[:, LINK : LINK + 1]
    kept_rows = side[:, KEEP : KEEP + 1].astype(F32)
    xe[:, 0:512] = x[...]
    xe[0:ROWS, 512:1024] = carry[...] * link[0:ROWS]
    if rows > ROWS:
        xe[ROWS:, 512:1024] = x[0 : rows - ROWS, :] * link[ROWS:]
    xe[:, 1024:1152] = side
    carry[...] = x[rows - ROWS :, :]
    carry_ids[...] = ids_now[:, rows - ROWS :]

    size = rows // subs
    for s in range(subs):
        at = slice(s * size, (s + 1) * size)
        up_all = nt_dot(res[at, :], o[:, 0:512]) + nt_dot(skp[at, :], o[:, 512:1024])
        for n in range(2):
            base = n * 2 * half
            pre = dot(xe[at, :], w[:, base : base + 2 * half])
            up = up_all[:, n * half : (n + 1) * half]
            filt = jnp.tanh(pre[:, :half])
            gate = 0.5 * jnp.tanh(0.5 * pre[:, half:]) + 0.5
            kept = kept_rows[at] * gate
            hidden = filt * kept
            hid[at, n * half : (n + 1) * half] = hidden.astype(BF)
            p[at, base : base + half] = (up * kept * (1.0 - filt * filt)).astype(BF)
            p[at, base + half : base + 2 * half] = (up * hidden * (1.0 - gate)).astype(BF)
    acc[...] += tn_dot(xe[...], p[...])
    acc_out[:, 0:512] += tn_dot(hid[...], res[...])
    acc_out[:, 512:1024] += tn_dot(hid[...], skp[...])
    for n, part in enumerate((res, skp)):
        total = jnp.sum(part[...].astype(F32), 0, keepdims=True)
        sums[:, n * 512 : (n + 1) * 512] += jnp.broadcast_to(total, (8, 512))

    @pl.when(step == 0)
    def _():
        past = nt_dot(p[0:ROWS, :], w[512:1024, :])
        edge[...] = (past * link[0:ROWS].astype(F32)).astype(BF)

    @pl.when(step == last)
    def _():
        if not split:
            grad[...] = acc[...]
            grad_out[...] = acc_out[...]
            return
        small[...] = jnp.zeros_like(small)
        for s in range(8):
            lane = mixed_block(s) * LANES
            small[s, 0:MEL, :] = acc[1024 : 1024 + MEL, lane : lane + LANES]
            for e in range(2):
                if s < 4:
                    lane = mixed_block(2 * s + e) * LANES
                    line = acc[1024 + ONES : 1024 + ONES + 1, lane : lane + LANES]
                else:
                    lane = (2 * (s - 4) + e) * LANES
                    line = sums[0:1, lane : lane + LANES]
                small[s, MEL + e : MEL + e + 1, :] = line

        def write(dest, shard, quarter):
            row = pl.multiple_of(64 * shard + TILE * quarter, TILE)
            put_tiles(dest, 0, acc[pl.ds(row, TILE), :], mixed_block)
            put_tiles(dest, 128, acc[pl.ds(512 + row, TILE), :], mixed_block)
            at = pl.multiple_of(32 * quarter, 32)
            dest[256:GATE_PART, :] = small[shard, pl.ds(at, 32), :].astype(dest.dtype)
            put_tiles(dest, GATE_PART, acc_out[pl.ds(row, TILE), :])

        emit_pieces((keep_out, send_out), write)


def gates_layer(split, rows, subs, x, tail, mel, keep, ids, tail_ids, res, skp, extra):
    total = x.shape[0]
    steps = total // rows
    by_row = lambda columns: pl.BlockSpec((rows, columns), lambda i: (i, 0))
    by_lane = lambda high: pl.BlockSpec((high, rows), lambda i: (0, i))
    in_specs = [
        by_row(512),
        whole((ROWS, 512)),
        by_lane(MEL),
        by_lane(1),
        by_lane(1),
        whole((1, ROWS)),
        by_row(512),
        by_row(512),
    ] + [ANY if split else whole(e.shape) for e in extra]
    out_specs = [
        by_row(1024),
        by_row(512),
        by_lane(TILE),
        whole((ROWS, 512)),
    ]
    out_shape = [
        jax.ShapeDtypeStruct((total, 1024), BF),
        jax.ShapeDtypeStruct((total, 512), BF),
        jax.ShapeDtypeStruct((TILE, total), BF),
        jax.ShapeDtypeStruct((ROWS, 512), BF),
    ]
    if split:
        more = [
            ((1024 + AUX, 1024), BF),
            ((512, 1024), BF),
            ((8, 1024), F32),
            ((4, 4, PART, LANES), BF),
            ((4, 4, PART, LANES), BF),
        ]
    else:
        more = [((1024 + AUX, 1024), F32), ((512, 1024), F32), ((8, 1024), F32)]
    for shape, dtype in more:
        out_specs.append(whole(shape))
        out_shape.append(jax.ShapeDtypeStruct(shape, dtype))
    scratch = [
        pltpu.VMEM((rows, 1024 + AUX), BF),
        pltpu.VMEM((ROWS, 512), BF),
        pltpu.VMEM((1, ROWS), jnp.int32),
        pltpu.VMEM((1024 + AUX, 1024), F32),
        pltpu.VMEM((512, 1024), F32),
    ]
    if split:
        scratch += [
            pltpu.VMEM((8, 1024), F32),
            pltpu.VMEM((8, AUX, LANES), F32),
            pltpu.VMEM((8, AUX, LANES), BF),
            pltpu.SemaphoreType.DMA((10,)),
        ]
        scratch += [pltpu.VMEM(e.shape, e.dtype) for e in extra[:10]]
    return pl.pallas_call(
        functools.partial(gates_body, split, subs),
        grid=(steps,),
        in_specs=in_specs,
        out_specs=out_specs,
        out_shape=out_shape,
        scratch_shapes=scratch,
        compiler_params=params(GATES_MIB),
        cost_estimate=cost(6.75 * 2 * total * 512 * 1024, total * 8000),
        name="gates_layer",
    )(x, tail, mel, keep, ids, tail_ids, res, skp, *extra)


def mixed_body(x, hid, o, bias, rest, edge, *refs):
    residual, skip, patch, token = refs[-4:]
    mixed = dot(hid[...], o[...]) + bias[0:1, :]
    residual[...] = (x[...].astype(F32) + mixed[:, 0:512]).astype(BF)
    skip[...] = mixed[:, 512:1024].astype(BF)

    @pl.when(pl.program_id(0) == 0)
    def _():
        patch[...] = (rest[...] + edge[...].astype(F32)).astype(BF)
        token[...] = jnp.zeros_like(token)


def mixed_layer(rows, x, hid, o, bias, rest, edge, input_grad, after):
    total = x.shape[0]
    by_row = pl.BlockSpec((rows, 512), lambda i: (i, 0))
    last = pl.BlockSpec((ROWS, 512), lambda i: (total // ROWS - 1, 0))
    operands = (x, hid, o, bias, rest, edge, input_grad, *after)
    return pl.pallas_call(
        mixed_body,
        grid=(total // rows,),
        in_specs=[by_row, by_row, whole((512, 1024)), whole((8, 1024)), whole((ROWS, 512)), whole((ROWS, 512))]
        + [ANY] * (1 + len(after)),
        out_specs=[by_row, by_row, last, whole(TOKEN.shape)],
        out_shape=[jax.ShapeDtypeStruct((total, 512), BF)] * 3 + [TOKEN],
        input_output_aliases={6: 2},
        compiler_params=params(58),
        cost_estimate=cost(2 * total * 512 * 1024, total * 4096),
        name="mixed_layer",
    )(*operands)


def input_body(res, p, flags, w, *refs):
    out, rest, token, carry = refs[-4:]
    step = pl.program_id(0)
    rows = res.shape[0]
    link = flags[...].T[:, LINK - MEL : LINK - MEL + 1].astype(F32)
    both = nt_dot(p[...], w[...])
    past = both[:, 512:1024] * link
    now = res[...].astype(F32) + both[:, 0:512]

    @pl.when(step == 0)
    def _():
        rest[...] = now[rows - ROWS :]
        carry[...] = jnp.zeros_like(carry)
        token[...] = jnp.zeros_like(token)

    if rows > ROWS:
        out[0 : rows - ROWS, :] = (now[0 : rows - ROWS] + past[ROWS:]).astype(BF)
    out[rows - ROWS :, :] = (now[rows - ROWS :] + carry[...]).astype(BF)
    carry[...] = past[0:ROWS]


def input_layer(rows, res, p, flags, w, after):
    total = res.shape[0]
    steps = total // rows
    by_row = lambda columns: pl.BlockSpec((rows, columns), lambda i: (steps - 1 - i, 0))
    return pl.pallas_call(
        input_body,
        grid=(steps,),
        in_specs=[
            by_row(512),
            by_row(1024),
            pl.BlockSpec((TILE, rows), lambda i: (0, steps - 1 - i)),
            pl.BlockSpec((1024, 1024), lambda i: (0, 0)),
        ]
        + [ANY] * len(after),
        out_specs=[by_row(512), whole((ROWS, 512)), whole(TOKEN.shape)],
        out_shape=[
            jax.ShapeDtypeStruct((total, 512), BF),
            jax.ShapeDtypeStruct((ROWS, 512), F32),
            TOKEN,
        ],
        scratch_shapes=[pltpu.VMEM((ROWS, 512), F32)],
        compiler_params=params(58),
        cost_estimate=cost(4 * total * 512 * 1024, total * 4096),
        name="input_layer",
    )(res, p, flags, w, *after)


def cores_body(keep, got, *outs):
    outs[4][...] = jnp.zeros_like(outs[4])
    for n in range(4):
        outs[n][...] = (keep[n].astype(F32) + got[n].astype(F32)).astype(outs[n].dtype)


def add_cores(keep, got):
    spec = pl.BlockSpec((4, 1, PART, LANES), lambda i: (0, i, 0, 0))
    return pl.pallas_call(
        cores_body,
        grid=(4,),
        in_specs=[spec, spec],
        out_specs=[pl.BlockSpec((1, PART, LANES), lambda i: (i, 0, 0))] * 4 + [whole(TOKEN.shape)],
        out_shape=[jax.ShapeDtypeStruct((4, PART, LANES), BF if n else F32) for n in range(4)] + [TOKEN],
        compiler_params=params(),
        cost_estimate=cost(10**6, 8 * 10**6),
        name="add_cores",
    )(keep, got)


def hop_body(keep, g1, g2, g3, *refs):
    outs = refs[-5:]
    outs[4][...] = jnp.zeros_like(outs[4])
    for n in range(4):
        total = keep[n] + g1[n].astype(F32) + g2[n].astype(F32) + g3[n].astype(F32)
        outs[n][...] = total.astype(outs[n].dtype)


def add_hop(parts, after):
    return pl.pallas_call(
        hop_body,
        in_specs=[VMEM] * 4 + [ANY] * len(after),
        out_specs=[VMEM] * 5,
        out_shape=[jax.ShapeDtypeStruct((PART, LANES), BF if n else F32) for n in range(4)] + [TOKEN],
        compiler_params=params(),
        cost_estimate=cost(10**6, 3 * 10**6),
        name="add_hop",
    )(*parts, *after)


def last_body(keep, g1, g2, g3, *refs):
    total, square = refs[-2:]
    total[...] = keep[...] + g1[...].astype(F32) + g2[...].astype(F32) + g3[...].astype(F32)
    square[...] = jnp.full(square.shape, jnp.sum(total[...] * total[...]), F32)


def add_last(parts, devices, after):
    return pl.pallas_call(
        last_body,
        in_specs=[VMEM] * 4 + [ANY] * len(after),
        out_specs=[VMEM] * 2,
        out_shape=[
            jax.ShapeDtypeStruct((PART, LANES), F32),
            jax.ShapeDtypeStruct((devices, LANES), F32),
        ],
        compiler_params=params(),
        cost_estimate=cost(10**6, 10**6),
        name="add_last",
    )(*parts, *after)


def adamw_update(grad, moment, second, weight, factor, decay):
    clipped = grad * factor
    moment_new = beta_one * moment + (1.0 - beta_one) * clipped
    second_new = beta_two * second + (1.0 - beta_two) * clipped * clipped
    mean_hat = moment_new / (1.0 - beta_one**STEP)
    square_hat = second_new / (1.0 - beta_two**STEP)
    weight_new = weight - learn_rate * (
        mean_hat / (jnp.sqrt(square_hat) + epsilon) + decay * weight
    )
    return (moment_new, second_new, weight_new)


def update_body(*refs):
    squares, parts = refs[0], refs[1:5]
    conv, cond, out, bias = refs[5:8], refs[8:11], refs[11:14], refs[14:17]
    norm, new, small = refs[17], refs[18:30], refs[30]
    _, rep, _ = spot()
    grad_norm = jnp.sqrt(jnp.sum(squares[...], 0, keepdims=True))
    norm[...] = grad_norm
    factor = clip_bound / jnp.maximum(grad_norm, clip_bound)

    def step(grad, old, dest, at, decay):
        got = adamw_update(grad, *[ref[at] for ref in old], factor, decay)
        for ref, value in zip(dest, got):
            ref[at] = value

    for k in range(4):
        row = pl.multiple_of((rep ^ k) * TILE, TILE)
        for b in range(8):
            lanes = slice(b * LANES, (b + 1) * LANES)
            for t in range(2):
                base = t * 128 + b * TILE
                step(parts[k][base : base + TILE, :], conv, new[0:3], (pl.ds(row, TILE), t, lanes), weight_decay)
            base = GATE_PART + b * TILE
            step(parts[k][base : base + TILE, :], out, new[6:9], (pl.ds(row, TILE), lanes), weight_decay)
        small[pl.ds(2 * row, 32), :] = parts[k][256:GATE_PART, :]
    step(small[0:MEL, :], cond, new[3:6], (slice(0, MEL), slice(0, LANES)), weight_decay)
    step(small[MEL : MEL + 2, :], bias, new[9:12], (slice(0, 2), slice(0, LANES)), 0.0)


def update(squares, parts, conv, cond, out, bias):
    shapes = [(1, LANES)]
    for group in (conv, cond, out, bias):
        shapes += [group[0].shape] * 3
    return pl.pallas_call(
        update_body,
        in_specs=[VMEM] * 17,
        out_specs=[VMEM] * 13,
        out_shape=[jax.ShapeDtypeStruct(s, F32) for s in shapes],
        scratch_shapes=[pltpu.VMEM((AUX, LANES), F32)],
        compiler_params=params(),
        name="update",
    )(squares, *parts, *conv, *cond, *out, *bias)


def local(
    inputs,
    mel_frames,
    utterance,
    keep_mask,
    res_grad,
    skip_grad,
    conv_weight,
    cond_weight,
    out_weight,
    biases,
    conv_first,
    conv_second,
    cond_first,
    cond_second,
    out_first,
    out_second,
    bias_first,
    bias_second,
):
    rows, width = inputs.shape
    span = DILATION_STEP
    split = lax.axis_size("rep") == 4 and lax.axis_size("seq") == 8
    tile = 1024

    if split:
        own, first = pack_weights(conv_weight, cond_weight, biases.reshape(2, LANES), out_weight)
        along = [swap(first, 0, 2 * j) for j in (1, 2, 3)]
        tail = from_behind(last_rows(inputs, along[0]), BOTH, 1)
        stack = jnp.concatenate(along, 0)
        here = (arrived_by(tail),)
        parts = across_hops(own, stack)
    else:
        w, o, bias_out = gather_plain(conv_weight, out_weight, cond_weight, biases)
        tail = from_behind(inputs[rows - span :], BOTH, 1)
        here = ()

    tail_ids = from_behind(utterance[rows - span :], BOTH, 1)
    samples = (
        inputs,
        tail,
        mel_frames,
        keep_mask.reshape(1, rows),
        utterance.reshape(1, rows),
        tail_ids.reshape(1, span),
        res_grad,
        skip_grad,
    )
    if split:
        p, hid, flags, edge, w, o, bias_out, keep, send = gates_layer(split, tile, 2, *samples, (*parts, *here))
        got = add_cores(keep, swap(send, 0, 1))
        part = [got[0]] + [swap(got[n], n, 0) for n in (1, 2, 3)]
        after = (got[4],)
    else:
        p, hid, flags, edge, grad, grad_out, sums = gates_layer(split, tile, 2, *samples, (w, o))
        after = ()

    returned = from_behind(edge, BOTH, -1)
    input_grad, rest, token = input_layer(tile, res_grad, p, flags, w, after)
    if split:
        got = add_hop(part, (token,))
        part = [got[0]] + [swap(got[n], 0, 2 * n) for n in (1, 2, 3)]
        after = (got[4],)
    residual_out, skip_out, input_grad, token = mixed_layer(
        tile, inputs, hid, o, bias_out, rest, returned, input_grad, after
    )

    if split:
        total, square = add_last(part, lax.axis_size(BOTH), (token,))
        part = [total] + [swap(total, n, 0) for n in (1, 2, 3)]
        squares = lax.all_to_all(square, BOTH, 0, 0, tiled=True)
        fold = lambda v: v.reshape(2, LANES)
        norm, *new = update(
            squares,
            part,
            (conv_first, conv_second, conv_weight),
            (cond_first, cond_second, cond_weight),
            (out_first, out_second, out_weight),
            (fold(bias_first), fold(bias_second), fold(biases)),
        )
        grad_norm = norm[0, 0]
        new = new[:9] + [v.reshape(-1) for v in new[9:]]
    else:
        grad = mixed_columns(grad)
        grad_conv = jnp.stack([grad[0:512], grad[512:1024]], 1)
        grad_bias = jnp.concatenate([grad[1024 + ONES], sums[0]], 0)
        own = (
            lax.psum_scatter(grad_conv, "seq", scatter_dimension=0, tiled=True),
            lax.psum_scatter(grad[1024 : 1024 + MEL], "seq", scatter_dimension=1, tiled=True),
            lax.psum_scatter(grad_out, "seq", scatter_dimension=0, tiled=True),
            lax.psum_scatter(grad_bias, "seq", scatter_dimension=0, tiled=True),
        )
        own = lax.psum(own, "rep")
        grad_norm = jnp.sqrt(lax.psum(sum(jnp.sum(g * g) for g in own), "seq"))
        factor = clip_bound / jnp.maximum(grad_norm, clip_bound)
        new = [
            *adamw_update(own[0], conv_first, conv_second, conv_weight, factor, weight_decay),
            *adamw_update(own[1], cond_first, cond_second, cond_weight, factor, weight_decay),
            *adamw_update(own[2], out_first, out_second, out_weight, factor, weight_decay),
            *adamw_update(own[3], bias_first, bias_second, biases, factor, 0.0),
        ]
    return (residual_out, skip_out, input_grad, grad_norm, *new)


def solution(mesh):
    rows = P(BOTH, None)
    line = P(BOTH)
    conv = P("seq", None, None)
    cond = P(None, "seq")
    out = P("seq", None)
    bias = P("seq")
    placed = (
        rows,
        P(None, BOTH),
        line,
        line,
        rows,
        rows,
        conv,
        cond,
        out,
        bias,
        conv,
        conv,
        cond,
        cond,
        out,
        out,
        bias,
        bias,
    )
    return jax.shard_map(
        local,
        mesh=mesh,
        in_specs=placed,
        out_specs=(rows, rows, rows, P()) + (conv,) * 3 + (cond,) * 3 + (out,) * 3 + (bias,) * 3,
        check_vma=False,
    )
```

```python
import functools

import jax
import jax.numpy as jnp
from jax import lax
from jax.experimental import pallas as pl
from jax.experimental.pallas import tpu as pltpu
from jax.sharding import PartitionSpec as P

DILATION_STEP = 512
STEP = 10

beta_one = 0.9
beta_two = 0.999
learn_rate = 0.05
weight_decay = 0.01
epsilon = 1e-08
clip_bound = 1.0

LANES = 128
TILE = 16
AUX = 128
MEL = 80
ONES = 80
KEEP = 81
LINK = 82
ROWS = 512
GATES_MIB = 52
ARRIVE = 10**10
BF = jnp.bfloat16
F32 = jnp.float32
BOTH = ("rep", "seq")


def from_behind(x, axis, by):
    count = lax.axis_size(axis)
    pairs = [(i, i + by) for i in range(count) if 0 <= i + by < count]
    return lax.ppermute(x, axis, pairs)


def swap(x, rep_bits, seq_bits):
    reps, seqs = lax.axis_size("rep"), lax.axis_size("seq")
    pairs = [
        (r * seqs + s, (r ^ rep_bits) * seqs + (s ^ seq_bits))
        for r in range(reps)
        for s in range(seqs)
    ]
    return lax.ppermute(x, BOTH, pairs)


def nt_dot(left, right):
    return lax.dot_general(
        left, right, (((1,), (1,)), ((), ())), preferred_element_type=F32
    )


def tn_dot(left, right):
    return lax.dot_general(
        left, right, (((0,), (0,)), ((), ())), preferred_element_type=F32
    )


def dot(left, right):
    return jnp.dot(left, right, preferred_element_type=F32)


TOKEN = jax.ShapeDtypeStruct((8, LANES), F32)


def params(mib=24):
    return pltpu.CompilerParams(vmem_limit_bytes=mib * 2**20)


def cost(flops, moved):
    return pl.CostEstimate(flops=int(flops), bytes_accessed=int(moved), transcendentals=0)


def whole(shape):
    return pl.BlockSpec(shape, lambda *_: (0,) * len(shape))


def spot():
    seq = lax.axis_index("seq")
    return seq % 2, lax.axis_index("rep"), seq // 2


VMEM = pl.BlockSpec(memory_space=pltpu.VMEM)
ANY = pl.BlockSpec(memory_space=pl.ANY)


OUT_PART = 8 * TILE
GATE_PART = 2 * 8 * TILE + 32
PART = GATE_PART + OUT_PART


def pack_body(conv, cond, bias, out, own, first, small):
    _, rep, _ = spot()
    small[0:MEL, :] = cond[...].astype(BF)
    small[MEL:96, :] = jnp.concatenate([bias[...], jnp.zeros((14, LANES), F32)], 0).astype(BF)
    small[96:AUX, :] = jnp.zeros((32, LANES), BF)
    for k in range(4):
        start = pl.multiple_of((rep ^ k) * TILE, TILE)
        for t in range(2):
            put_tiles(own.at[k], t * 128, conv[pl.ds(start, TILE), t, :])
        own[k, 256:GATE_PART, :] = small[pl.ds(2 * start, 32), :]
        put_tiles(own.at[k], GATE_PART, out[pl.ds(start, TILE), :])
    first[...] = own[0]


def pack_weights(conv, cond, bias, out):
    return pl.pallas_call(
        pack_body,
        in_specs=[VMEM] * 4,
        out_specs=[VMEM] * 2,
        out_shape=[
            jax.ShapeDtypeStruct((4, PART, LANES), BF),
            jax.ShapeDtypeStruct((PART, LANES), BF),
        ],
        scratch_shapes=[pltpu.VMEM((AUX, LANES), BF)],
        compiler_params=params(58),
        name="pack_weights",
    )(conv, cond, bias, out)


def tail_body(x, _, tail):
    tail[...] = x[...]


def last_rows(x, after):
    return pl.pallas_call(
        tail_body,
        grid=(1,),
        in_specs=[pl.BlockSpec((ROWS, x.shape[1]), lambda i: (x.shape[0] // ROWS - 1, 0)), ANY],
        out_specs=whole((ROWS, x.shape[1])),
        out_shape=jax.ShapeDtypeStruct((ROWS, x.shape[1]), x.dtype),
        compiler_params=params(58),
        name="last_rows",
    )(x, after)


def flags_body(keep, ids, tail_ids, _, flags):
    first = jnp.where(lax.axis_index(BOTH) > 0, tail_ids[...], -1)
    past = jnp.concatenate([first, ids[:, 0 : ids.shape[1] - ROWS]], 1)
    place = lax.broadcasted_iota(jnp.int32, flags.shape, 0)
    link = jnp.where(place == LINK - ONES, (ids[...] == past).astype(F32), 0.0)
    kept = jnp.where(place == KEEP - ONES, keep[...].astype(F32), link)
    flags[...] = jnp.where(place == 0, 1.0, kept).astype(BF)


def flag_rows(keep, ids, tail_ids, after):
    return pl.pallas_call(
        flags_body,
        in_specs=[VMEM] * 3 + [ANY],
        out_specs=VMEM,
        out_shape=jax.ShapeDtypeStruct((TILE, keep.shape[1]), BF),
        compiler_params=params(),
        cost_estimate=cost(ARRIVE, 4096),
        name="flag_rows",
    )(keep, ids, tail_ids, after)


def mixed_block(block):
    low, mid, top = block & 1, (block >> 1) & 1, (block >> 2) & 1
    return low + 4 * mid + 2 * top


def each_part(own, stack, sides, write):
    core, rep, z = spot()
    for c in range(2):
        for j in range(4):
            for k in range(4):
                if j == 0:
                    source = own[c].at[k]
                elif k == 0:
                    source = stack[c].at[pl.ds((j - 1) * PART, PART), :]
                else:
                    source = sides[c][k - 1].at[pl.ds((j - 1) * PART, PART), :]
                write(source, 2 * (z ^ j) + (core ^ c), rep ^ k)


def unpack(refs, w, o, bias_out, small):
    def write(source, shard, quarter):
        row = pl.multiple_of(64 * shard + TILE * quarter, TILE)
        for b in range(8):
            lanes = pl.ds(mixed_block(b) * LANES, LANES)
            w[pl.ds(row, TILE), lanes] = source[b * TILE : (b + 1) * TILE, :]
            w[pl.ds(512 + row, TILE), lanes] = source[128 + b * TILE : 128 + (b + 1) * TILE, :]
        small[shard, pl.ds(pl.multiple_of(32 * quarter, 32), 32), :] = source[256:GATE_PART, :]
        for b in range(8):
            base = GATE_PART + b * TILE
            o[pl.ds(row, TILE), b * LANES : (b + 1) * LANES] = source[base : base + TILE, :]

    each_part(refs[0:2], refs[2:4], (refs[4:7], refs[7:10]), write)
    blank = jnp.zeros((TILE - 1, LANES), BF)
    for s in range(8):
        lane = mixed_block(s) * LANES
        w[1024 : 1024 + MEL, lane : lane + LANES] = small[s, 0:MEL, :]
        tail = small[s, MEL : MEL + TILE, :]
        for e in range(2):
            if s < 4:
                at = mixed_block(2 * s + e) * LANES
                w[1104:1120, at : at + LANES] = jnp.concatenate([tail[e : e + 1], blank], 0)
            else:
                at = (2 * (s - 4) + e) * LANES
                bias_out[:, at : at + LANES] = jnp.broadcast_to(tail[e : e + 1].astype(F32), (8, LANES))
    w[1120:1152, :] = jnp.zeros((32, w.shape[1]), BF)


def across_hops(own, stack):
    across = [swap(stack, k, 0) for k in (1, 2, 3)]
    return [own, swap(own, 0, 1), stack, swap(stack, 0, 1), *across, *[swap(a, 0, 1) for a in across]]


def mixed_columns(x):
    rows, columns = x.shape
    return x.reshape(rows, 2, 2, columns // 4).transpose(0, 2, 1, 3).reshape(rows, columns)


def gather_plain(conv_weight, out_weight, cond_weight, biases):
    conv = conv_weight.astype(BF).transpose(1, 0, 2)
    conv_all = lax.all_gather(conv, "seq", axis=1, tiled=True)
    cond_all = lax.all_gather(cond_weight.astype(BF), "seq", axis=1, tiled=True)
    out_all = lax.all_gather(out_weight.astype(BF), "seq", axis=0, tiled=True)
    bias_all = lax.all_gather(biases.astype(BF), "seq", axis=0, tiled=True)
    gates = cond_all.shape[1]
    w = jnp.concatenate(
        [
            conv_all[0],
            conv_all[1],
            cond_all,
            bias_all[None, :gates],
            jnp.zeros((AUX - MEL - 1, gates), BF),
        ],
        0,
    )
    bias_out = jnp.broadcast_to(bias_all[None, gates:].astype(F32), (8, gates))
    return mixed_columns(w), out_all, bias_out


def emit_pieces(outs, write):
    core, rep, z = spot()
    for c, dest in enumerate(outs):

        def one(n, carry, c=c, dest=dest):
            k, j = n // 4, n % 4
            write(dest.at[k, j], 2 * (z ^ j) + (core ^ c), rep ^ k)
            return carry

        lax.fori_loop(0, 16, one, 0)


def put_tiles(dest, base, value, order=lambda b: b):
    value = value.astype(dest.dtype)
    for b in range(value.shape[1] // LANES):
        lane = order(b) * LANES
        dest[base + b * TILE : base + (b + 1) * TILE, :] = value[:, lane : lane + LANES]


def gates_body(split, subs, x, tail, mel, flags, res, skp, *refs):
    if split:
        parts, refs = refs[0:10], refs[10:]
        p, hid, edge, w, o, bias_out, keep_out, send_out = refs[:8]
        xe, carry, acc, acc_out, sums, small, small_low, arrived, *held = refs[8:]
    else:
        w, o, p, hid, edge, grad, grad_out, sums, xe, carry, acc, acc_out = refs
    step, last = pl.program_id(0), pl.num_programs(0) - 1
    rows, half = x.shape[0], p.shape[1] // 4

    @pl.when(step == 0)
    def _():
        carry[...] = tail[...]
        acc[...] = jnp.zeros_like(acc)
        acc_out[...] = jnp.zeros_like(acc_out)
        sums[...] = jnp.zeros_like(sums)
        if split:
            copies = [
                pltpu.make_async_copy(part, here, arrived.at[n])
                for n, (part, here) in enumerate(zip(parts, held))
            ]
            for copy in copies:
                copy.start()
            for copy in copies:
                copy.wait()
            unpack(held, w, o, bias_out, small_low)

    side = jnp.concatenate([mel[...], flags[...], jnp.zeros((32, rows), BF)], 0).T
    link = side[:, LINK : LINK + 1]
    kept_rows = side[:, KEEP : KEEP + 1].astype(F32)
    xe[:, 0:512] = x[...]
    xe[0:ROWS, 512:1024] = carry[...] * link[0:ROWS]
    if rows > ROWS:
        xe[ROWS:, 512:1024] = x[0 : rows - ROWS, :] * link[ROWS:]
    xe[:, 1024:1152] = side
    carry[...] = x[rows - ROWS :, :]

    size = rows // subs
    for s in range(subs):
        at = slice(s * size, (s + 1) * size)
        up_all = nt_dot(res[at, :], o[:, 0:512]) + nt_dot(skp[at, :], o[:, 512:1024])
        for n in range(2):
            base = n * 2 * half
            pre = dot(xe[at, :], w[:, base : base + 2 * half])
            up = up_all[:, n * half : (n + 1) * half]
            filt = jnp.tanh(pre[:, :half])
            gate = 0.5 * jnp.tanh(0.5 * pre[:, half:]) + 0.5
            kept = kept_rows[at] * gate
            hidden = filt * kept
            hid[at, n * half : (n + 1) * half] = hidden.astype(BF)
            p[at, base : base + half] = (up * kept * (1.0 - filt * filt)).astype(BF)
            p[at, base + half : base + 2 * half] = (up * hidden * (1.0 - gate)).astype(BF)
    acc[...] += tn_dot(xe[...], p[...])
    left = jnp.concatenate([hid[...], side[:, MEL : MEL + TILE]], 1)
    got = tn_dot(left, jnp.concatenate([res[...], skp[...]], 1))
    acc_out[...] += got[0:512]
    sums[...] += got[512:520]

    @pl.when(step == 0)
    def _():
        past = nt_dot(p[0:ROWS, :], w[512:1024, :])
        edge[...] = (past * link[0:ROWS].astype(F32)).astype(BF)

    @pl.when(step == last)
    def _():
        if not split:
            grad[...] = acc[...]
            grad_out[...] = acc_out[...]
            return
        small[...] = jnp.zeros_like(small)
        for s in range(8):
            lane = mixed_block(s) * LANES
            small[s, 0:MEL, :] = acc[1024 : 1024 + MEL, lane : lane + LANES]
            for e in range(2):
                if s < 4:
                    lane = mixed_block(2 * s + e) * LANES
                    line = acc[1024 + ONES : 1024 + ONES + 1, lane : lane + LANES]
                else:
                    lane = (2 * (s - 4) + e) * LANES
                    line = sums[0:1, lane : lane + LANES]
                small[s, MEL + e : MEL + e + 1, :] = line

        def write(dest, shard, quarter):
            row = pl.multiple_of(64 * shard + TILE * quarter, TILE)
            put_tiles(dest, 0, acc[pl.ds(row, TILE), :], mixed_block)
            put_tiles(dest, 128, acc[pl.ds(512 + row, TILE), :], mixed_block)
            at = pl.multiple_of(32 * quarter, 32)
            dest[256:GATE_PART, :] = small[shard, pl.ds(at, 32), :].astype(dest.dtype)
            put_tiles(dest, GATE_PART, acc_out[pl.ds(row, TILE), :])

        emit_pieces((keep_out, send_out), write)


def gates_layer(split, rows, subs, x, tail, mel, flags, res, skp, extra):
    total = x.shape[0]
    steps = total // rows
    by_row = lambda columns: pl.BlockSpec((rows, columns), lambda i: (i, 0))
    by_lane = lambda high: pl.BlockSpec((high, rows), lambda i: (0, i))
    in_specs = [
        by_row(512),
        whole((ROWS, 512)),
        by_lane(MEL),
        by_lane(TILE),
        by_row(512),
        by_row(512),
    ] + [ANY if split else whole(e.shape) for e in extra]
    out_specs = [
        by_row(1024),
        by_row(512),
        whole((ROWS, 512)),
    ]
    out_shape = [
        jax.ShapeDtypeStruct((total, 1024), BF),
        jax.ShapeDtypeStruct((total, 512), BF),
        jax.ShapeDtypeStruct((ROWS, 512), BF),
    ]
    if split:
        more = [
            ((1024 + AUX, 1024), BF),
            ((512, 1024), BF),
            ((8, 1024), F32),
            ((4, 4, PART, LANES), BF),
            ((4, 4, PART, LANES), BF),
        ]
    else:
        more = [((1024 + AUX, 1024), F32), ((512, 1024), F32), ((8, 1024), F32)]
    for shape, dtype in more:
        out_specs.append(whole(shape))
        out_shape.append(jax.ShapeDtypeStruct(shape, dtype))
    scratch = [
        pltpu.VMEM((rows, 1024 + AUX), BF),
        pltpu.VMEM((ROWS, 512), BF),
        pltpu.VMEM((1024 + AUX, 1024), F32),
        pltpu.VMEM((512, 1024), F32),
    ]
    if split:
        scratch += [
            pltpu.VMEM((8, 1024), F32),
            pltpu.VMEM((8, AUX, LANES), F32),
            pltpu.VMEM((8, AUX, LANES), BF),
            pltpu.SemaphoreType.DMA((10,)),
        ]
        scratch += [pltpu.VMEM(e.shape, e.dtype) for e in extra]
    return pl.pallas_call(
        functools.partial(gates_body, split, subs),
        grid=(steps,),
        in_specs=in_specs,
        out_specs=out_specs,
        out_shape=out_shape,
        scratch_shapes=scratch,
        compiler_params=params(GATES_MIB),
        cost_estimate=cost(6.75 * 2 * total * 512 * 1024, total * 8000),
        name="gates_layer",
    )(x, tail, mel, flags, res, skp, *extra)


def mixed_body(x, hid, o, bias, *refs):
    residual, skip, token = refs[-3:]
    mixed = dot(hid[...], o[...]) + bias[0:1, :]
    residual[...] = (x[...].astype(F32) + mixed[:, 0:512]).astype(BF)
    skip[...] = mixed[:, 512:1024].astype(BF)

    @pl.when(pl.program_id(0) == 0)
    def _():
        token[...] = jnp.zeros_like(token)


def patch_body(x, hid, o, bias, rest, edge, *refs):
    residual, skip, patch, token = refs[-4:]
    mixed_body(x, hid, o, bias, residual, skip, token)

    @pl.when(pl.program_id(0) == 0)
    def _():
        patch[...] = (rest[...] + edge[...].astype(F32)).astype(BF)


def mixed_layer(rows, first, steps, x, hid, o, bias, patched, partial, after):
    total = x.shape[0]
    by_row = pl.BlockSpec((rows, 512), lambda i: (first + i, 0))
    last = pl.BlockSpec((ROWS, 512), lambda i: (total // ROWS - 1, 0))
    operands = [x, hid, o, bias]
    in_specs = [by_row, by_row, whole((512, 1024)), whole((8, 1024))]
    out_specs = [by_row, by_row]
    aliases = {}
    if patched:
        rest, edge, input_grad = patched
        operands += [rest, edge, input_grad]
        in_specs += [whole((ROWS, 512)), whole((ROWS, 512)), ANY]
        out_specs.append(last)
        aliases[6] = 2
    for n, array in enumerate(partial):
        aliases[len(operands)] = n
        operands.append(array)
        in_specs.append(ANY)
    return pl.pallas_call(
        patch_body if patched else mixed_body,
        grid=(steps,),
        in_specs=in_specs + [ANY] * len(after),
        out_specs=out_specs + [whole(TOKEN.shape)],
        out_shape=[jax.ShapeDtypeStruct((total, 512), BF)] * len(out_specs) + [TOKEN],
        input_output_aliases=aliases,
        compiler_params=params(58),
        cost_estimate=cost(2 * rows * steps * 512 * 1024, rows * steps * 4096),
        name="mixed_layer_%d" % first,
    )(*operands, *after)


def input_body(res, p, flags, w, *refs):
    out, rest, token, carry = refs[-4:]
    step = pl.program_id(0)
    rows = res.shape[0]
    link = flags[...].T[:, LINK - MEL : LINK - MEL + 1].astype(F32)
    both = nt_dot(p[...], w[...])
    past = both[:, 512:1024] * link
    now = res[...].astype(F32) + both[:, 0:512]

    @pl.when(step == 0)
    def _():
        rest[...] = now[rows - ROWS :]
        carry[...] = jnp.zeros_like(carry)
        token[...] = jnp.zeros_like(token)

    if rows > ROWS:
        out[0 : rows - ROWS, :] = (now[0 : rows - ROWS] + past[ROWS:]).astype(BF)
    out[rows - ROWS :, :] = (now[rows - ROWS :] + carry[...]).astype(BF)
    carry[...] = past[0:ROWS]


def input_layer(rows, res, p, flags, w, after):
    total = res.shape[0]
    steps = total // rows
    by_row = lambda columns: pl.BlockSpec((rows, columns), lambda i: (steps - 1 - i, 0))
    return pl.pallas_call(
        input_body,
        grid=(steps,),
        in_specs=[
            by_row(512),
            by_row(1024),
            pl.BlockSpec((TILE, rows), lambda i: (0, steps - 1 - i)),
            pl.BlockSpec((1024, 1024), lambda i: (0, 0)),
        ]
        + [ANY] * len(after),
        out_specs=[by_row(512), whole((ROWS, 512)), whole(TOKEN.shape)],
        out_shape=[
            jax.ShapeDtypeStruct((total, 512), BF),
            jax.ShapeDtypeStruct((ROWS, 512), F32),
            TOKEN,
        ],
        scratch_shapes=[pltpu.VMEM((ROWS, 512), F32)],
        compiler_params=params(58),
        cost_estimate=cost(4 * total * 512 * 1024, total * 4096),
        name="input_layer",
    )(res, p, flags, w, *after)


def cores_body(keep, got, *outs):
    for n in range(4):
        outs[n][...] = (keep[n].astype(F32) + got[n].astype(F32)).astype(outs[n].dtype)


def add_cores(keep, got):
    spec = pl.BlockSpec((4, 1, PART, LANES), lambda i: (0, i, 0, 0))
    return pl.pallas_call(
        cores_body,
        grid=(4,),
        in_specs=[spec, spec],
        out_specs=[pl.BlockSpec((1, PART, LANES), lambda i: (i, 0, 0))] * 4,
        out_shape=[jax.ShapeDtypeStruct((4, PART, LANES), BF if n else F32) for n in range(4)],
        compiler_params=params(),
        cost_estimate=cost(10**6, 8 * 10**6),
        name="add_cores",
    )(keep, got)


def hop_body(keep, g1, g2, g3, *refs):
    outs = refs[-5:]
    outs[4][...] = jnp.zeros_like(outs[4])
    for n in range(4):
        total = keep[n] + g1[n].astype(F32) + g2[n].astype(F32) + g3[n].astype(F32)
        outs[n][...] = total.astype(outs[n].dtype)


def add_hop(parts, after):
    return pl.pallas_call(
        hop_body,
        in_specs=[VMEM] * 4 + [ANY] * len(after),
        out_specs=[VMEM] * 5,
        out_shape=[jax.ShapeDtypeStruct((PART, LANES), BF if n else F32) for n in range(4)] + [TOKEN],
        compiler_params=params(),
        cost_estimate=cost(10**6, 3 * 10**6),
        name="add_hop",
    )(*parts, *after)


def last_body(keep, g1, g2, g3, *refs):
    total, square = refs[-2:]
    total[...] = keep[...] + g1[...].astype(F32) + g2[...].astype(F32) + g3[...].astype(F32)
    square[...] = jnp.full(square.shape, jnp.sum(total[...] * total[...]), F32)


def add_last(parts, devices, after):
    return pl.pallas_call(
        last_body,
        in_specs=[VMEM] * 4 + [ANY] * len(after),
        out_specs=[VMEM] * 2,
        out_shape=[
            jax.ShapeDtypeStruct((PART, LANES), F32),
            jax.ShapeDtypeStruct((devices, LANES), F32),
        ],
        compiler_params=params(),
        cost_estimate=cost(10**6, 10**6),
        name="add_last",
    )(*parts, *after)


def adamw_update(grad, moment, second, weight, factor, decay):
    clipped = grad * factor
    moment_new = beta_one * moment + (1.0 - beta_one) * clipped
    second_new = beta_two * second + (1.0 - beta_two) * clipped * clipped
    mean_hat = moment_new / (1.0 - beta_one**STEP)
    square_hat = second_new / (1.0 - beta_two**STEP)
    weight_new = weight - learn_rate * (
        mean_hat / (jnp.sqrt(square_hat) + epsilon) + decay * weight
    )
    return (moment_new, second_new, weight_new)


def update_body(*refs):
    squares, parts = refs[0], refs[1:5]
    conv, cond, out, bias = refs[5:8], refs[8:11], refs[11:14], refs[14:17]
    norm, new, small = refs[17], refs[18:30], refs[30]
    _, rep, _ = spot()
    grad_norm = jnp.sqrt(jnp.sum(squares[...], 0, keepdims=True))
    norm[...] = grad_norm
    factor = clip_bound / jnp.maximum(grad_norm, clip_bound)

    def step(grad, old, dest, at, decay):
        got = adamw_update(grad, *[ref[at] for ref in old], factor, decay)
        for ref, value in zip(dest, got):
            ref[at] = value

    for k in range(4):
        row = pl.multiple_of((rep ^ k) * TILE, TILE)
        for b in range(8):
            lanes = slice(b * LANES, (b + 1) * LANES)
            for t in range(2):
                base = t * 128 + b * TILE
                step(parts[k][base : base + TILE, :], conv, new[0:3], (pl.ds(row, TILE), t, lanes), weight_decay)
            base = GATE_PART + b * TILE
            step(parts[k][base : base + TILE, :], out, new[6:9], (pl.ds(row, TILE), lanes), weight_decay)
        small[pl.ds(2 * row, 32), :] = parts[k][256:GATE_PART, :]
    step(small[0:MEL, :], cond, new[3:6], (slice(0, MEL), slice(0, LANES)), weight_decay)
    step(small[MEL : MEL + 2, :], bias, new[9:12], (slice(0, 2), slice(0, LANES)), 0.0)


def update(squares, parts, conv, cond, out, bias):
    shapes = [(1, LANES)]
    for group in (conv, cond, out, bias):
        shapes += [group[0].shape] * 3
    return pl.pallas_call(
        update_body,
        in_specs=[VMEM] * 17,
        out_specs=[VMEM] * 13,
        out_shape=[jax.ShapeDtypeStruct(s, F32) for s in shapes],
        scratch_shapes=[pltpu.VMEM((AUX, LANES), F32)],
        compiler_params=params(),
        name="update",
    )(squares, *parts, *conv, *cond, *out, *bias)


def local(
    inputs,
    mel_frames,
    utterance,
    keep_mask,
    res_grad,
    skip_grad,
    conv_weight,
    cond_weight,
    out_weight,
    biases,
    conv_first,
    conv_second,
    cond_first,
    cond_second,
    out_first,
    out_second,
    bias_first,
    bias_second,
):
    rows, width = inputs.shape
    span = DILATION_STEP
    split = lax.axis_size("rep") == 4 and lax.axis_size("seq") == 8
    tile = 1024

    if split:
        own, first = pack_weights(conv_weight, cond_weight, biases.reshape(2, LANES), out_weight)
        along = [swap(first, 0, 2 * j) for j in (1, 2, 3)]
        tail = from_behind(last_rows(inputs, along[0]), BOTH, 1)
        stack = jnp.concatenate(along, 0)
        parts = across_hops(own, stack)
    else:
        w, o, bias_out = gather_plain(conv_weight, out_weight, cond_weight, biases)
        tail = from_behind(inputs[rows - span :], BOTH, 1)

    tail_ids = from_behind(utterance[rows - span :], BOTH, 1)
    flags = flag_rows(
        keep_mask.reshape(1, rows), utterance.reshape(1, rows), tail_ids.reshape(1, span), tail
    )
    samples = (inputs, tail, mel_frames, flags, res_grad, skip_grad)
    if split:
        p, hid, edge, w, o, bias_out, keep, send = gates_layer(split, tile, 2, *samples, parts)
        got = add_cores(keep, swap(send, 0, 1))
        part = [got[0]] + [swap(got[n], n, 0) for n in (1, 2, 3)]
        after = (got[1],)
    else:
        p, hid, edge, grad, grad_out, sums = gates_layer(split, tile, 2, *samples, (w, o))
        after = ()

    returned = from_behind(edge, BOTH, -1)
    input_grad, rest, token = input_layer(tile, res_grad, p, flags, w, after)
    if split:
        got = add_hop(part, (token,))
        part = [got[0]] + [swap(got[n], 0, 2 * n) for n in (1, 2, 3)]
        after = (got[4],)
    steps = rows // tile
    cut = steps * 4 // 6
    mixed = functools.partial(mixed_layer, tile)
    *sample_outs, token = mixed(0, cut, inputs, hid, o, bias_out, (), (), after)
    if split:
        total, square = add_last(part, lax.axis_size(BOTH), (token,))
        after = (square,)
    residual_out, skip_out, input_grad, _ = mixed(
        cut, steps - cut, inputs, hid, o, bias_out, (rest, returned, input_grad), sample_outs, after
    )

    if split:
        part = [total] + [swap(total, n, 0) for n in (1, 2, 3)]
        squares = lax.all_to_all(square, BOTH, 0, 0, tiled=True)
        fold = lambda v: v.reshape(2, LANES)
        norm, *new = update(
            squares,
            part,
            (conv_first, conv_second, conv_weight),
            (cond_first, cond_second, cond_weight),
            (out_first, out_second, out_weight),
            (fold(bias_first), fold(bias_second), fold(biases)),
        )
        grad_norm = norm[0, 0]
        new = new[:9] + [v.reshape(-1) for v in new[9:]]
    else:
        grad = mixed_columns(grad)
        grad_conv = jnp.stack([grad[0:512], grad[512:1024]], 1)
        grad_bias = jnp.concatenate([grad[1024 + ONES], sums[0]], 0)
        own = (
            lax.psum_scatter(grad_conv, "seq", scatter_dimension=0, tiled=True),
            lax.psum_scatter(grad[1024 : 1024 + MEL], "seq", scatter_dimension=1, tiled=True),
            lax.psum_scatter(grad_out, "seq", scatter_dimension=0, tiled=True),
            lax.psum_scatter(grad_bias, "seq", scatter_dimension=0, tiled=True),
        )
        own = lax.psum(own, "rep")
        grad_norm = jnp.sqrt(lax.psum(sum(jnp.sum(g * g) for g in own), "seq"))
        factor = clip_bound / jnp.maximum(grad_norm, clip_bound)
        new = [
            *adamw_update(own[0], conv_first, conv_second, conv_weight, factor, weight_decay),
            *adamw_update(own[1], cond_first, cond_second, cond_weight, factor, weight_decay),
            *adamw_update(own[2], out_first, out_second, out_weight, factor, weight_decay),
            *adamw_update(own[3], bias_first, bias_second, biases, factor, 0.0),
        ]
    return (residual_out, skip_out, input_grad, grad_norm, *new)


def solution(mesh):
    rows = P(BOTH, None)
    line = P(BOTH)
    conv = P("seq", None, None)
    cond = P(None, "seq")
    out = P("seq", None)
    bias = P("seq")
    placed = (
        rows,
        P(None, BOTH),
        line,
        line,
        rows,
        rows,
        conv,
        cond,
        out,
        bias,
        conv,
        conv,
        cond,
        cond,
        out,
        out,
        bias,
        bias,
    )
    return jax.shard_map(
        local,
        mesh=mesh,
        in_specs=placed,
        out_specs=(rows, rows, rows, P()) + (conv,) * 3 + (cond,) * 3 + (out,) * 3 + (bias,) * 3,
        check_vma=False,
    )
```

```python
import functools

import jax
import jax.numpy as jnp
from jax import lax
from jax.experimental import pallas as pl
from jax.experimental.pallas import tpu as pltpu
from jax.sharding import PartitionSpec as P

DILATION_STEP = 512
STEP = 10

beta_one = 0.9
beta_two = 0.999
learn_rate = 0.05
weight_decay = 0.01
epsilon = 1e-08
clip_bound = 1.0

LANES = 128
TILE = 16
AUX = 128
MEL = 80
ONES = 80
KEEP = 81
LINK = 82
ROWS = 512
GATES_MIB = 45
ARRIVE = 10**10
BF = jnp.bfloat16
F32 = jnp.float32
BOTH = ("rep", "seq")


def from_behind(x, axis, by):
    count = lax.axis_size(axis)
    pairs = [(i, i + by) for i in range(count) if 0 <= i + by < count]
    return lax.ppermute(x, axis, pairs)


def swap(x, rep_bits, seq_bits):
    reps, seqs = lax.axis_size("rep"), lax.axis_size("seq")
    pairs = [
        (r * seqs + s, (r ^ rep_bits) * seqs + (s ^ seq_bits))
        for r in range(reps)
        for s in range(seqs)
    ]
    return lax.ppermute(x, BOTH, pairs)


def nt_dot(left, right):
    return lax.dot_general(
        left, right, (((1,), (1,)), ((), ())), preferred_element_type=F32
    )


def tn_dot(left, right):
    return lax.dot_general(
        left, right, (((0,), (0,)), ((), ())), preferred_element_type=F32
    )


def dot(left, right):
    return jnp.dot(left, right, preferred_element_type=F32)


TOKEN = jax.ShapeDtypeStruct((8, LANES), F32)


def params(mib=24):
    return pltpu.CompilerParams(vmem_limit_bytes=mib * 2**20)


def cost(flops, moved):
    return pl.CostEstimate(flops=int(flops), bytes_accessed=int(moved), transcendentals=0)


def whole(shape):
    return pl.BlockSpec(shape, lambda *_: (0,) * len(shape))


def spot():
    seq = lax.axis_index("seq")
    return seq % 2, lax.axis_index("rep"), seq // 2


VMEM = pl.BlockSpec(memory_space=pltpu.VMEM)
ANY = pl.BlockSpec(memory_space=pl.ANY)


OUT_PART = 8 * TILE
GATE_PART = 2 * 8 * TILE + 32
PART = GATE_PART + OUT_PART


def pack_body(conv, cond, bias, out, own, first, small):
    _, rep, _ = spot()
    small[0:MEL, :] = cond[...].astype(BF)
    small[MEL:96, :] = jnp.concatenate([bias[...], jnp.zeros((14, LANES), F32)], 0).astype(BF)
    small[96:AUX, :] = jnp.zeros((32, LANES), BF)
    for k in range(4):
        start = pl.multiple_of((rep ^ k) * TILE, TILE)
        for t in range(2):
            put_tiles(own.at[k], t * 128, conv[pl.ds(start, TILE), t, :])
        own[k, 256:GATE_PART, :] = small[pl.ds(2 * start, 32), :]
        put_tiles(own.at[k], GATE_PART, out[pl.ds(start, TILE), :])
    first[...] = own[0]


def pack_weights(conv, cond, bias, out):
    return pl.pallas_call(
        pack_body,
        in_specs=[VMEM] * 4,
        out_specs=[VMEM] * 2,
        out_shape=[
            jax.ShapeDtypeStruct((4, PART, LANES), BF),
            jax.ShapeDtypeStruct((PART, LANES), BF),
        ],
        scratch_shapes=[pltpu.VMEM((AUX, LANES), BF)],
        compiler_params=params(58),
        name="pack_weights",
    )(conv, cond, bias, out)


def tail_body(x, _, tail):
    tail[...] = x[...]


def last_rows(x, after):
    return pl.pallas_call(
        tail_body,
        grid=(1,),
        in_specs=[pl.BlockSpec((ROWS, x.shape[1]), lambda i: (x.shape[0] // ROWS - 1, 0)), ANY],
        out_specs=whole((ROWS, x.shape[1])),
        out_shape=jax.ShapeDtypeStruct((ROWS, x.shape[1]), x.dtype),
        compiler_params=params(58),
        name="last_rows",
    )(x, after)


def flags_body(keep, ids, tail_ids, _, flags):
    first = jnp.where(lax.axis_index(BOTH) > 0, tail_ids[...], -1)
    past = jnp.concatenate([first, ids[:, 0 : ids.shape[1] - ROWS]], 1)
    place = lax.broadcasted_iota(jnp.int32, flags.shape, 0)
    link = jnp.where(place == LINK - ONES, (ids[...] == past).astype(F32), 0.0)
    kept = jnp.where(place == KEEP - ONES, keep[...].astype(F32), link)
    flags[...] = jnp.where(place == 0, 1.0, kept).astype(BF)


def flag_rows(keep, ids, tail_ids, after):
    return pl.pallas_call(
        flags_body,
        in_specs=[VMEM] * 3 + [ANY],
        out_specs=VMEM,
        out_shape=jax.ShapeDtypeStruct((TILE, keep.shape[1]), BF),
        compiler_params=params(),
        cost_estimate=cost(ARRIVE, 4096),
        name="flag_rows",
    )(keep, ids, tail_ids, after)


def mixed_block(block):
    low, mid, top = block & 1, (block >> 1) & 1, (block >> 2) & 1
    return low + 4 * mid + 2 * top


def each_part(own, stack, sides, write):
    core, rep, z = spot()
    for c in range(2):
        for j in range(4):
            for k in range(4):
                if j == 0:
                    source = own[c].at[k]
                elif k == 0:
                    source = stack[c].at[pl.ds((j - 1) * PART, PART), :]
                else:
                    source = sides[c][k - 1].at[pl.ds((j - 1) * PART, PART), :]
                write(source, 2 * (z ^ j) + (core ^ c), rep ^ k)


def unpack(refs, w, o, bias_out, small):
    def write(source, shard, quarter):
        row = pl.multiple_of(64 * shard + TILE * quarter, TILE)
        for b in range(8):
            lanes = pl.ds(mixed_block(b) * LANES, LANES)
            w[pl.ds(row, TILE), lanes] = source[b * TILE : (b + 1) * TILE, :]
            w[pl.ds(512 + row, TILE), lanes] = source[128 + b * TILE : 128 + (b + 1) * TILE, :]
        small[shard, pl.ds(pl.multiple_of(32 * quarter, 32), 32), :] = source[256:GATE_PART, :]
        for b in range(8):
            base = GATE_PART + b * TILE
            o[pl.ds(row, TILE), b * LANES : (b + 1) * LANES] = source[base : base + TILE, :]

    each_part(refs[0:2], refs[2:4], (refs[4:7], refs[7:10]), write)
    blank = jnp.zeros((TILE - 1, LANES), BF)
    for s in range(8):
        lane = mixed_block(s) * LANES
        w[1024 : 1024 + MEL, lane : lane + LANES] = small[s, 0:MEL, :]
        tail = small[s, MEL : MEL + TILE, :]
        for e in range(2):
            if s < 4:
                at = mixed_block(2 * s + e) * LANES
                w[1104:1120, at : at + LANES] = jnp.concatenate([tail[e : e + 1], blank], 0)
            else:
                at = (2 * (s - 4) + e) * LANES
                bias_out[:, at : at + LANES] = jnp.broadcast_to(tail[e : e + 1].astype(F32), (8, LANES))
    w[1120:1152, :] = jnp.zeros((32, w.shape[1]), BF)


def across_hops(own, stack):
    across = [swap(stack, k, 0) for k in (1, 2, 3)]
    return [own, swap(own, 0, 1), stack, swap(stack, 0, 1), *across, *[swap(a, 0, 1) for a in across]]


def mixed_columns(x):
    rows, columns = x.shape
    return x.reshape(rows, 2, 2, columns // 4).transpose(0, 2, 1, 3).reshape(rows, columns)


def gather_plain(conv_weight, out_weight, cond_weight, biases):
    conv = conv_weight.astype(BF).transpose(1, 0, 2)
    conv_all = lax.all_gather(conv, "seq", axis=1, tiled=True)
    cond_all = lax.all_gather(cond_weight.astype(BF), "seq", axis=1, tiled=True)
    out_all = lax.all_gather(out_weight.astype(BF), "seq", axis=0, tiled=True)
    bias_all = lax.all_gather(biases.astype(BF), "seq", axis=0, tiled=True)
    gates = cond_all.shape[1]
    w = jnp.concatenate(
        [
            conv_all[0],
            conv_all[1],
            cond_all,
            bias_all[None, :gates],
            jnp.zeros((AUX - MEL - 1, gates), BF),
        ],
        0,
    )
    bias_out = jnp.broadcast_to(bias_all[None, gates:].astype(F32), (8, gates))
    return mixed_columns(w), out_all, bias_out


def emit_pieces(outs, write):
    core, rep, z = spot()
    for c, dest in enumerate(outs):

        def one(n, carry, c=c, dest=dest):
            k, j = n // 4, n % 4
            write(dest.at[k, j], 2 * (z ^ j) + (core ^ c), rep ^ k)
            return carry

        lax.fori_loop(0, 16, one, 0)


def put_tiles(dest, base, value, order=lambda b: b):
    value = value.astype(dest.dtype)
    for b in range(value.shape[1] // LANES):
        lane = order(b) * LANES
        dest[base + b * TILE : base + (b + 1) * TILE, :] = value[:, lane : lane + LANES]


def gates_body(split, subs, x, tail, mel, flags, res, skp, *refs):
    if split:
        parts, refs = refs[0:10], refs[10:]
        p, hid, edge, w, o, bias_out, keep_out, send_out = refs[:8]
        xe, carry, acc, acc_out, sums, small, small_low, arrived, *held = refs[8:]
    else:
        w, o, p, hid, edge, grad, grad_out, sums, xe, carry, acc, acc_out = refs
    step, last = pl.program_id(0), pl.num_programs(0) - 1
    rows, half = x.shape[0], p.shape[1] // 4

    @pl.when(step == 0)
    def _():
        carry[...] = tail[...]
        acc[...] = jnp.zeros_like(acc)
        acc_out[...] = jnp.zeros_like(acc_out)
        sums[...] = jnp.zeros_like(sums)
        if split:
            copies = [
                pltpu.make_async_copy(part, here, arrived.at[n])
                for n, (part, here) in enumerate(zip(parts, held))
            ]
            for copy in copies:
                copy.start()
            for copy in copies:
                copy.wait()
            unpack(held, w, o, bias_out, small_low)

    side = jnp.concatenate([mel[...], flags[...], jnp.zeros((32, rows), BF)], 0).T
    link = side[:, LINK : LINK + 1]
    kept_rows = side[:, KEEP : KEEP + 1].astype(F32)
    xe[:, 0:512] = x[...]
    xe[0:ROWS, 512:1024] = carry[...] * link[0:ROWS]
    if rows > ROWS:
        xe[ROWS:, 512:1024] = x[0 : rows - ROWS, :] * link[ROWS:]
    xe[:, 1024:1152] = side
    carry[...] = x[rows - ROWS :, :]

    size = rows // subs
    for s in range(subs):
        at = slice(s * size, (s + 1) * size)
        up_all = nt_dot(res[at, :], o[:, 0:512]) + nt_dot(skp[at, :], o[:, 512:1024])
        for n in range(2):
            base = n * 2 * half
            pre = dot(xe[at, :], w[:, base : base + 2 * half])
            up = up_all[:, n * half : (n + 1) * half]
            filt = jnp.tanh(pre[:, :half])
            gate = 0.5 * jnp.tanh(0.5 * pre[:, half:]) + 0.5
            kept = kept_rows[at] * gate
            hidden = filt * kept
            hid[at, n * half : (n + 1) * half] = hidden.astype(BF)
            p[at, base : base + half] = (up * kept * (1.0 - filt * filt)).astype(BF)
            p[at, base + half : base + 2 * half] = (up * hidden * (1.0 - gate)).astype(BF)
    acc[...] += tn_dot(xe[...], p[...])
    left = jnp.concatenate([hid[...], side[:, MEL : MEL + TILE]], 1)
    got = tn_dot(left, jnp.concatenate([res[...], skp[...]], 1))
    acc_out[...] += got[0:512]
    sums[...] += got[512:520]

    @pl.when(step == 0)
    def _():
        past = nt_dot(p[0:ROWS, :], w[512:1024, :])
        edge[...] = (past * link[0:ROWS].astype(F32)).astype(BF)

    @pl.when(step == last)
    def _():
        if not split:
            grad[...] = acc[...]
            grad_out[...] = acc_out[...]
            return
        small[...] = jnp.zeros_like(small)
        for s in range(8):
            lane = mixed_block(s) * LANES
            small[s, 0:MEL, :] = acc[1024 : 1024 + MEL, lane : lane + LANES]
            for e in range(2):
                if s < 4:
                    lane = mixed_block(2 * s + e) * LANES
                    line = acc[1024 + ONES : 1024 + ONES + 1, lane : lane + LANES]
                else:
                    lane = (2 * (s - 4) + e) * LANES
                    line = sums[0:1, lane : lane + LANES]
                small[s, MEL + e : MEL + e + 1, :] = line

        def write(dest, shard, quarter):
            row = pl.multiple_of(64 * shard + TILE * quarter, TILE)
            put_tiles(dest, 0, acc[pl.ds(row, TILE), :], mixed_block)
            put_tiles(dest, 128, acc[pl.ds(512 + row, TILE), :], mixed_block)
            at = pl.multiple_of(32 * quarter, 32)
            dest[256:GATE_PART, :] = small[shard, pl.ds(at, 32), :].astype(dest.dtype)
            put_tiles(dest, GATE_PART, acc_out[pl.ds(row, TILE), :])

        emit_pieces((keep_out, send_out), write)


def gates_layer(split, rows, subs, x, tail, mel, flags, res, skp, extra):
    total = x.shape[0]
    steps = total // rows
    by_row = lambda columns: pl.BlockSpec((rows, columns), lambda i: (i, 0))
    by_lane = lambda high: pl.BlockSpec((high, rows), lambda i: (0, i))
    in_specs = [
        by_row(512),
        whole((ROWS, 512)),
        by_lane(MEL),
        by_lane(TILE),
        by_row(512),
        by_row(512),
    ] + [ANY if split else whole(e.shape) for e in extra]
    out_specs = [
        by_row(1024),
        by_row(512),
        whole((ROWS, 512)),
    ]
    out_shape = [
        jax.ShapeDtypeStruct((total, 1024), BF),
        jax.ShapeDtypeStruct((total, 512), BF),
        jax.ShapeDtypeStruct((ROWS, 512), BF),
    ]
    if split:
        more = [
            ((1024 + AUX, 1024), BF),
            ((512, 1024), BF),
            ((8, 1024), F32),
            ((4, 4, PART, LANES), BF),
            ((4, 4, PART, LANES), BF),
        ]
    else:
        more = [((1024 + AUX, 1024), F32), ((512, 1024), F32), ((8, 1024), F32)]
    for shape, dtype in more:
        out_specs.append(whole(shape))
        out_shape.append(jax.ShapeDtypeStruct(shape, dtype))
    scratch = [
        pltpu.VMEM((rows, 1024 + AUX), BF),
        pltpu.VMEM((ROWS, 512), BF),
        pltpu.VMEM((1024 + AUX, 1024), F32),
        pltpu.VMEM((512, 1024), F32),
    ]
    if split:
        scratch += [
            pltpu.VMEM((8, 1024), F32),
            pltpu.VMEM((8, AUX, LANES), F32),
            pltpu.VMEM((8, AUX, LANES), BF),
            pltpu.SemaphoreType.DMA((10,)),
        ]
        scratch += [pltpu.VMEM(e.shape, e.dtype) for e in extra]
    return pl.pallas_call(
        functools.partial(gates_body, split, subs),
        grid=(steps,),
        in_specs=in_specs,
        out_specs=out_specs,
        out_shape=out_shape,
        scratch_shapes=scratch,
        compiler_params=params(GATES_MIB),
        cost_estimate=cost(6.75 * 2 * total * 512 * 1024, total * 8000),
        name="gates_layer",
    )(x, tail, mel, flags, res, skp, *extra)


def mixed_body(x, hid, o, bias, *refs):
    residual, skip, token = refs[-3:]
    mixed = dot(hid[...], o[...]) + bias[0:1, :]
    residual[...] = (x[...].astype(F32) + mixed[:, 0:512]).astype(BF)
    skip[...] = mixed[:, 512:1024].astype(BF)

    @pl.when(pl.program_id(0) == 0)
    def _():
        token[...] = jnp.zeros_like(token)


def patch_body(x, hid, o, bias, rest, edge, *refs):
    residual, skip, patch, token = refs[-4:]
    mixed_body(x, hid, o, bias, residual, skip, token)

    @pl.when(pl.program_id(0) == 0)
    def _():
        patch[...] = (rest[...] + edge[...].astype(F32)).astype(BF)


def mixed_layer(rows, first, steps, x, hid, o, bias, patched, partial, after):
    total = x.shape[0]
    by_row = pl.BlockSpec((rows, 512), lambda i: (first + i, 0))
    last = pl.BlockSpec((ROWS, 512), lambda i: (total // ROWS - 1, 0))
    operands = [x, hid, o, bias]
    in_specs = [by_row, by_row, whole((512, 1024)), whole((8, 1024))]
    out_specs = [by_row, by_row]
    aliases = {}
    if patched:
        rest, edge, input_grad = patched
        operands += [rest, edge, input_grad]
        in_specs += [whole((ROWS, 512)), whole((ROWS, 512)), ANY]
        out_specs.append(last)
        aliases[6] = 2
    for n, array in enumerate(partial):
        aliases[len(operands)] = n
        operands.append(array)
        in_specs.append(ANY)
    return pl.pallas_call(
        patch_body if patched else mixed_body,
        grid=(steps,),
        in_specs=in_specs + [ANY] * len(after),
        out_specs=out_specs + [whole(TOKEN.shape)],
        out_shape=[jax.ShapeDtypeStruct((total, 512), BF)] * len(out_specs) + [TOKEN],
        input_output_aliases=aliases,
        compiler_params=params(58),
        cost_estimate=cost(2 * rows * steps * 512 * 1024, rows * steps * 4096),
        name="mixed_layer_%d" % first,
    )(*operands, *after)


def input_body(res, p, flags, w, *refs):
    out, rest, token, carry = refs[-4:]
    step = pl.program_id(0)
    rows = res.shape[0]
    link = flags[...].T[:, LINK - MEL : LINK - MEL + 1].astype(F32)
    both = nt_dot(p[...], w[...])
    past = both[:, 512:1024] * link
    now = res[...].astype(F32) + both[:, 0:512]

    @pl.when(step == 0)
    def _():
        rest[...] = now[rows - ROWS :]
        carry[...] = jnp.zeros_like(carry)
        token[...] = jnp.zeros_like(token)

    if rows > ROWS:
        out[0 : rows - ROWS, :] = (now[0 : rows - ROWS] + past[ROWS:]).astype(BF)
    out[rows - ROWS :, :] = (now[rows - ROWS :] + carry[...]).astype(BF)
    carry[...] = past[0:ROWS]


def input_layer(rows, res, p, flags, w, after):
    total = res.shape[0]
    steps = total // rows
    by_row = lambda columns: pl.BlockSpec((rows, columns), lambda i: (steps - 1 - i, 0))
    return pl.pallas_call(
        input_body,
        grid=(steps,),
        in_specs=[
            by_row(512),
            by_row(1024),
            pl.BlockSpec((TILE, rows), lambda i: (0, steps - 1 - i)),
            pl.BlockSpec((1024, 1024), lambda i: (0, 0)),
        ]
        + [ANY] * len(after),
        out_specs=[by_row(512), whole((ROWS, 512)), whole(TOKEN.shape)],
        out_shape=[
            jax.ShapeDtypeStruct((total, 512), BF),
            jax.ShapeDtypeStruct((ROWS, 512), F32),
            TOKEN,
        ],
        scratch_shapes=[pltpu.VMEM((ROWS, 512), F32)],
        compiler_params=params(58),
        cost_estimate=cost(4 * total * 512 * 1024, total * 4096),
        name="input_layer",
    )(res, p, flags, w, *after)


def cores_body(keep, got, *outs):
    for n in range(4):
        outs[n][...] = (keep[n].astype(F32) + got[n].astype(F32)).astype(outs[n].dtype)


def add_cores(keep, got):
    spec = pl.BlockSpec((4, 1, PART, LANES), lambda i: (0, i, 0, 0))
    return pl.pallas_call(
        cores_body,
        grid=(4,),
        in_specs=[spec, spec],
        out_specs=[pl.BlockSpec((1, PART, LANES), lambda i: (i, 0, 0))] * 4,
        out_shape=[jax.ShapeDtypeStruct((4, PART, LANES), BF if n else F32) for n in range(4)],
        compiler_params=params(),
        cost_estimate=cost(10**6, 8 * 10**6),
        name="add_cores",
    )(keep, got)


def hop_body(keep, g1, g2, g3, *refs):
    outs = refs[-5:]
    outs[4][...] = jnp.zeros_like(outs[4])
    for n in range(4):
        total = keep[n] + g1[n].astype(F32) + g2[n].astype(F32) + g3[n].astype(F32)
        outs[n][...] = total.astype(outs[n].dtype)


def add_hop(parts, after):
    return pl.pallas_call(
        hop_body,
        in_specs=[VMEM] * 4 + [ANY] * len(after),
        out_specs=[VMEM] * 5,
        out_shape=[jax.ShapeDtypeStruct((PART, LANES), BF if n else F32) for n in range(4)] + [TOKEN],
        compiler_params=params(),
        cost_estimate=cost(10**6, 3 * 10**6),
        name="add_hop",
    )(*parts, *after)


def last_body(keep, g1, g2, g3, *refs):
    total, square = refs[-2:]
    total[...] = keep[...] + g1[...].astype(F32) + g2[...].astype(F32) + g3[...].astype(F32)
    square[...] = jnp.full(square.shape, jnp.sum(total[...] * total[...]), F32)


def add_last(parts, devices, after):
    return pl.pallas_call(
        last_body,
        in_specs=[VMEM] * 4 + [ANY] * len(after),
        out_specs=[VMEM] * 2,
        out_shape=[
            jax.ShapeDtypeStruct((PART, LANES), F32),
            jax.ShapeDtypeStruct((devices, LANES), F32),
        ],
        compiler_params=params(),
        cost_estimate=cost(10**6, 10**6),
        name="add_last",
    )(*parts, *after)


def adamw_update(grad, moment, second, weight, factor, decay):
    clipped = grad * factor
    moment_new = beta_one * moment + (1.0 - beta_one) * clipped
    second_new = beta_two * second + (1.0 - beta_two) * clipped * clipped
    mean_hat = moment_new / (1.0 - beta_one**STEP)
    square_hat = second_new / (1.0 - beta_two**STEP)
    weight_new = weight - learn_rate * (
        mean_hat / (jnp.sqrt(square_hat) + epsilon) + decay * weight
    )
    return (moment_new, second_new, weight_new)


def update_body(*refs):
    squares, parts = refs[0], refs[1:5]
    conv, cond, out, bias = refs[5:8], refs[8:11], refs[11:14], refs[14:17]
    norm, new, small = refs[17], refs[18:30], refs[30]
    _, rep, _ = spot()
    grad_norm = jnp.sqrt(jnp.sum(squares[...], 0, keepdims=True))
    norm[...] = grad_norm
    factor = clip_bound / jnp.maximum(grad_norm, clip_bound)

    def step(grad, old, dest, at, decay):
        got = adamw_update(grad, *[ref[at] for ref in old], factor, decay)
        for ref, value in zip(dest, got):
            ref[at] = value

    for k in range(4):
        row = pl.multiple_of((rep ^ k) * TILE, TILE)
        for b in range(8):
            lanes = slice(b * LANES, (b + 1) * LANES)
            for t in range(2):
                base = t * 128 + b * TILE
                step(parts[k][base : base + TILE, :], conv, new[0:3], (pl.ds(row, TILE), t, lanes), weight_decay)
            base = GATE_PART + b * TILE
            step(parts[k][base : base + TILE, :], out, new[6:9], (pl.ds(row, TILE), lanes), weight_decay)
        small[pl.ds(2 * row, 32), :] = parts[k][256:GATE_PART, :]
    step(small[0:MEL, :], cond, new[3:6], (slice(0, MEL), slice(0, LANES)), weight_decay)
    step(small[MEL : MEL + 2, :], bias, new[9:12], (slice(0, 2), slice(0, LANES)), 0.0)


def update(squares, parts, conv, cond, out, bias):
    shapes = [(1, LANES)]
    for group in (conv, cond, out, bias):
        shapes += [group[0].shape] * 3
    return pl.pallas_call(
        update_body,
        in_specs=[VMEM] * 17,
        out_specs=[VMEM] * 13,
        out_shape=[jax.ShapeDtypeStruct(s, F32) for s in shapes],
        scratch_shapes=[pltpu.VMEM((AUX, LANES), F32)],
        compiler_params=params(),
        name="update",
    )(squares, *parts, *conv, *cond, *out, *bias)


def local(
    inputs,
    mel_frames,
    utterance,
    keep_mask,
    res_grad,
    skip_grad,
    conv_weight,
    cond_weight,
    out_weight,
    biases,
    conv_first,
    conv_second,
    cond_first,
    cond_second,
    out_first,
    out_second,
    bias_first,
    bias_second,
):
    rows, width = inputs.shape
    span = DILATION_STEP
    split = lax.axis_size("rep") == 4 and lax.axis_size("seq") == 8
    tile = 1024

    if split:
        own, first = pack_weights(conv_weight, cond_weight, biases.reshape(2, LANES), out_weight)
        along = [swap(first, 0, 2 * j) for j in (1, 2, 3)]
        tail = from_behind(last_rows(inputs, along[0]), BOTH, 1)
        stack = jnp.concatenate(along, 0)
        parts = across_hops(own, stack)
    else:
        w, o, bias_out = gather_plain(conv_weight, out_weight, cond_weight, biases)
        tail = from_behind(inputs[rows - span :], BOTH, 1)

    tail_ids = from_behind(utterance[rows - span :], BOTH, 1)
    flags = flag_rows(
        keep_mask.reshape(1, rows), utterance.reshape(1, rows), tail_ids.reshape(1, span), tail
    )
    samples = (inputs, tail, mel_frames, flags, res_grad, skip_grad)
    if split:
        p, hid, edge, w, o, bias_out, keep, send = gates_layer(split, tile, 2, *samples, parts)
        got = add_cores(keep, swap(send, 0, 1))
        part = [got[0]] + [swap(got[n], n, 0) for n in (1, 2, 3)]
        after = (got[1],)
    else:
        p, hid, edge, grad, grad_out, sums = gates_layer(split, tile, 2, *samples, (w, o))
        after = ()

    returned = from_behind(edge, BOTH, -1)
    input_grad, rest, token = input_layer(tile, res_grad, p, flags, w, after)
    if split:
        got = add_hop(part, (token,))
        part = [got[0]] + [swap(got[n], 0, 2 * n) for n in (1, 2, 3)]
        after = (got[4],)
    steps = rows // tile
    cut = steps * 4 // 6
    mixed = functools.partial(mixed_layer, tile)
    *sample_outs, token = mixed(0, cut, inputs, hid, o, bias_out, (), (), after)
    if split:
        total, square = add_last(part, lax.axis_size(BOTH), (token,))
        after = (square,)
    residual_out, skip_out, input_grad, _ = mixed(
        cut, steps - cut, inputs, hid, o, bias_out, (rest, returned, input_grad), sample_outs, after
    )

    if split:
        part = [total] + [swap(total, n, 0) for n in (1, 2, 3)]
        squares = lax.all_to_all(square, BOTH, 0, 0, tiled=True)
        fold = lambda v: v.reshape(2, LANES)
        norm, *new = update(
            squares,
            part,
            (conv_first, conv_second, conv_weight),
            (cond_first, cond_second, cond_weight),
            (out_first, out_second, out_weight),
            (fold(bias_first), fold(bias_second), fold(biases)),
        )
        grad_norm = norm[0, 0]
        new = new[:9] + [v.reshape(-1) for v in new[9:]]
    else:
        grad = mixed_columns(grad)
        grad_conv = jnp.stack([grad[0:512], grad[512:1024]], 1)
        grad_bias = jnp.concatenate([grad[1024 + ONES], sums[0]], 0)
        own = (
            lax.psum_scatter(grad_conv, "seq", scatter_dimension=0, tiled=True),
            lax.psum_scatter(grad[1024 : 1024 + MEL], "seq", scatter_dimension=1, tiled=True),
            lax.psum_scatter(grad_out, "seq", scatter_dimension=0, tiled=True),
            lax.psum_scatter(grad_bias, "seq", scatter_dimension=0, tiled=True),
        )
        own = lax.psum(own, "rep")
        grad_norm = jnp.sqrt(lax.psum(sum(jnp.sum(g * g) for g in own), "seq"))
        factor = clip_bound / jnp.maximum(grad_norm, clip_bound)
        new = [
            *adamw_update(own[0], conv_first, conv_second, conv_weight, factor, weight_decay),
            *adamw_update(own[1], cond_first, cond_second, cond_weight, factor, weight_decay),
            *adamw_update(own[2], out_first, out_second, out_weight, factor, weight_decay),
            *adamw_update(own[3], bias_first, bias_second, biases, factor, 0.0),
        ]
    return (residual_out, skip_out, input_grad, grad_norm, *new)


def solution(mesh):
    rows = P(BOTH, None)
    line = P(BOTH)
    conv = P("seq", None, None)
    cond = P(None, "seq")
    out = P("seq", None)
    bias = P("seq")
    placed = (
        rows,
        P(None, BOTH),
        line,
        line,
        rows,
        rows,
        conv,
        cond,
        out,
        bias,
        conv,
        conv,
        cond,
        cond,
        out,
        out,
        bias,
        bias,
    )
    return jax.shard_map(
        local,
        mesh=mesh,
        in_specs=placed,
        out_specs=(rows, rows, rows, P()) + (conv,) * 3 + (cond,) * 3 + (out,) * 3 + (bias,) * 3,
        check_vma=False,
    )
```

```python
import functools

import jax
import jax.numpy as jnp
from jax import lax
from jax.experimental import pallas as pl
from jax.experimental.pallas import tpu as pltpu
from jax.sharding import PartitionSpec as P

DILATION_STEP = 512
STEP = 10

beta_one = 0.9
beta_two = 0.999
learn_rate = 0.05
weight_decay = 0.01
epsilon = 1e-08
clip_bound = 1.0

LANES = 128
TILE = 16
AUX = 128
MEL = 80
ONES = 80
KEEP = 81
LINK = 82
ROWS = 512
GATES_MIB = 45
ARRIVE = 10**10
BF = jnp.bfloat16
F32 = jnp.float32
BOTH = ("rep", "seq")


def from_behind(x, axis, by):
    count = lax.axis_size(axis)
    pairs = [(i, i + by) for i in range(count) if 0 <= i + by < count]
    return lax.ppermute(x, axis, pairs)


def swap(x, rep_bits, seq_bits):
    reps, seqs = lax.axis_size("rep"), lax.axis_size("seq")
    pairs = [
        (r * seqs + s, (r ^ rep_bits) * seqs + (s ^ seq_bits))
        for r in range(reps)
        for s in range(seqs)
    ]
    return lax.ppermute(x, BOTH, pairs)


def nt_dot(left, right):
    return lax.dot_general(
        left, right, (((1,), (1,)), ((), ())), preferred_element_type=F32
    )


def tn_dot(left, right):
    return lax.dot_general(
        left, right, (((0,), (0,)), ((), ())), preferred_element_type=F32
    )


def dot(left, right):
    return jnp.dot(left, right, preferred_element_type=F32)


TOKEN = jax.ShapeDtypeStruct((8, LANES), F32)


def params(mib=24):
    return pltpu.CompilerParams(vmem_limit_bytes=mib * 2**20)


def cost(flops, moved):
    return pl.CostEstimate(flops=int(flops), bytes_accessed=int(moved), transcendentals=0)


def whole(shape):
    return pl.BlockSpec(shape, lambda *_: (0,) * len(shape))


def spot():
    seq = lax.axis_index("seq")
    return seq % 2, lax.axis_index("rep"), seq // 2


VMEM = pl.BlockSpec(memory_space=pltpu.VMEM)
ANY = pl.BlockSpec(memory_space=pl.ANY)


OUT_PART = 8 * TILE
GATE_PART = 2 * 8 * TILE + 32
PART = GATE_PART + OUT_PART


def pack_body(conv, cond, bias, out, own, first, small):
    _, rep, _ = spot()
    small[0:MEL, :] = cond[...].astype(BF)
    small[MEL:96, :] = jnp.concatenate([bias[...], jnp.zeros((14, LANES), F32)], 0).astype(BF)
    small[96:AUX, :] = jnp.zeros((32, LANES), BF)
    for k in range(4):
        start = pl.multiple_of((rep ^ k) * TILE, TILE)
        for t in range(2):
            put_tiles(own.at[k], t * 128, conv[pl.ds(start, TILE), t, :])
        own[k, 256:GATE_PART, :] = small[pl.ds(2 * start, 32), :]
        put_tiles(own.at[k], GATE_PART, out[pl.ds(start, TILE), :])
    first[...] = own[0]


def pack_weights(conv, cond, bias, out):
    return pl.pallas_call(
        pack_body,
        in_specs=[VMEM] * 4,
        out_specs=[VMEM] * 2,
        out_shape=[
            jax.ShapeDtypeStruct((4, PART, LANES), BF),
            jax.ShapeDtypeStruct((PART, LANES), BF),
        ],
        scratch_shapes=[pltpu.VMEM((AUX, LANES), BF)],
        compiler_params=params(58),
        name="pack_weights",
    )(conv, cond, bias, out)


def tail_body(x, _, tail):
    tail[...] = x[...]


def last_rows(x, after):
    return pl.pallas_call(
        tail_body,
        grid=(1,),
        in_specs=[pl.BlockSpec((ROWS, x.shape[1]), lambda i: (x.shape[0] // ROWS - 1, 0)), ANY],
        out_specs=whole((ROWS, x.shape[1])),
        out_shape=jax.ShapeDtypeStruct((ROWS, x.shape[1]), x.dtype),
        compiler_params=params(58),
        name="last_rows",
    )(x, after)


def flags_body(keep, ids, tail_ids, _, flags):
    first = jnp.where(lax.axis_index(BOTH) > 0, tail_ids[...], -1)
    past = jnp.concatenate([first, ids[:, 0 : ids.shape[1] - ROWS]], 1)
    place = lax.broadcasted_iota(jnp.int32, flags.shape, 0)
    link = jnp.where(place == LINK - ONES, (ids[...] == past).astype(F32), 0.0)
    kept = jnp.where(place == KEEP - ONES, keep[...].astype(F32), link)
    flags[...] = jnp.where(place == 0, 1.0, kept).astype(BF)


def flag_rows(keep, ids, tail_ids, after):
    return pl.pallas_call(
        flags_body,
        in_specs=[VMEM] * 3 + [ANY],
        out_specs=VMEM,
        out_shape=jax.ShapeDtypeStruct((TILE, keep.shape[1]), BF),
        compiler_params=params(),
        cost_estimate=cost(ARRIVE, 4096),
        name="flag_rows",
    )(keep, ids, tail_ids, after)


def mixed_block(block):
    low, mid, top = block & 1, (block >> 1) & 1, (block >> 2) & 1
    return low + 4 * mid + 2 * top


def each_part(own, stack, sides, write):
    core, rep, z = spot()
    for c in range(2):
        for j in range(4):
            for k in range(4):
                if j == 0:
                    source = own[c].at[k]
                elif k == 0:
                    source = stack[c].at[pl.ds((j - 1) * PART, PART), :]
                else:
                    source = sides[c][k - 1].at[pl.ds((j - 1) * PART, PART), :]
                write(source, 2 * (z ^ j) + (core ^ c), rep ^ k)


def unpack(refs, w, o, bias_out, small):
    def write(source, shard, quarter):
        row = pl.multiple_of(64 * shard + TILE * quarter, TILE)
        for b in range(8):
            lanes = pl.ds(mixed_block(b) * LANES, LANES)
            w[pl.ds(row, TILE), lanes] = source[b * TILE : (b + 1) * TILE, :]
            w[pl.ds(512 + row, TILE), lanes] = source[128 + b * TILE : 128 + (b + 1) * TILE, :]
        small[shard, pl.ds(pl.multiple_of(32 * quarter, 32), 32), :] = source[256:GATE_PART, :]
        for b in range(8):
            base = GATE_PART + b * TILE
            o[pl.ds(row, TILE), b * LANES : (b + 1) * LANES] = source[base : base + TILE, :]

    each_part(refs[0:2], refs[2:4], (refs[4:7], refs[7:10]), write)
    blank = jnp.zeros((TILE - 1, LANES), BF)
    for s in range(8):
        lane = mixed_block(s) * LANES
        w[1024 : 1024 + MEL, lane : lane + LANES] = small[s, 0:MEL, :]
        tail = small[s, MEL : MEL + TILE, :]
        for e in range(2):
            if s < 4:
                at = mixed_block(2 * s + e) * LANES
                w[1104:1120, at : at + LANES] = jnp.concatenate([tail[e : e + 1], blank], 0)
            else:
                at = (2 * (s - 4) + e) * LANES
                bias_out[:, at : at + LANES] = jnp.broadcast_to(tail[e : e + 1].astype(F32), (8, LANES))
    w[1120:1152, :] = jnp.zeros((32, w.shape[1]), BF)


def across_hops(own, stack):
    across = [swap(stack, k, 0) for k in (1, 2, 3)]
    return [own, swap(own, 0, 1), stack, swap(stack, 0, 1), *across, *[swap(a, 0, 1) for a in across]]


def mixed_columns(x):
    rows, columns = x.shape
    return x.reshape(rows, 2, 2, columns // 4).transpose(0, 2, 1, 3).reshape(rows, columns)


def gather_plain(conv_weight, out_weight, cond_weight, biases):
    conv = conv_weight.astype(BF).transpose(1, 0, 2)
    conv_all = lax.all_gather(conv, "seq", axis=1, tiled=True)
    cond_all = lax.all_gather(cond_weight.astype(BF), "seq", axis=1, tiled=True)
    out_all = lax.all_gather(out_weight.astype(BF), "seq", axis=0, tiled=True)
    bias_all = lax.all_gather(biases.astype(BF), "seq", axis=0, tiled=True)
    gates = cond_all.shape[1]
    w = jnp.concatenate(
        [
            conv_all[0],
            conv_all[1],
            cond_all,
            bias_all[None, :gates],
            jnp.zeros((AUX - MEL - 1, gates), BF),
        ],
        0,
    )
    bias_out = jnp.broadcast_to(bias_all[None, gates:].astype(F32), (8, gates))
    return mixed_columns(w), out_all, bias_out


def emit_pieces(outs, write):
    core, rep, z = spot()
    for c, dest in enumerate(outs):

        def one(n, carry, c=c, dest=dest):
            k, j = n // 4, n % 4
            write(dest.at[k, j], 2 * (z ^ j) + (core ^ c), rep ^ k)
            return carry

        lax.fori_loop(0, 16, one, 0)


def put_tiles(dest, base, value, order=lambda b: b):
    value = value.astype(dest.dtype)
    for b in range(value.shape[1] // LANES):
        lane = order(b) * LANES
        dest[base + b * TILE : base + (b + 1) * TILE, :] = value[:, lane : lane + LANES]


def gates_body(split, subs, x, tail, mel, flags, res, skp, *refs):
    if split:
        parts, refs = refs[0:10], refs[10:]
        p, hid, edge, w_out, o_out, bias_out, keep_out, send_out = refs[:8]
        xe, carry, acc, acc_out, sums, small, small_low, w, o, arrived, *held = refs[8:]
        passed = [
            pltpu.make_async_copy(w, w_out, arrived.at[10]),
            pltpu.make_async_copy(o, o_out, arrived.at[11]),
        ]
    else:
        w, o, p, hid, edge, grad, grad_out, sums, xe, carry, acc, acc_out = refs
    step, last = pl.program_id(0), pl.num_programs(0) - 1
    rows, half = x.shape[0], p.shape[1] // 4

    @pl.when(step == 0)
    def _():
        carry[...] = tail[...]
        acc[...] = jnp.zeros_like(acc)
        acc_out[...] = jnp.zeros_like(acc_out)
        sums[...] = jnp.zeros_like(sums)
        if split:
            copies = [
                pltpu.make_async_copy(part, here, arrived.at[n])
                for n, (part, here) in enumerate(zip(parts, held))
            ]
            for copy in copies:
                copy.start()
            for copy in copies:
                copy.wait()
            unpack(held, w, o, bias_out, small_low)
            for copy in passed:
                copy.start()

    side = jnp.concatenate([mel[...], flags[...], jnp.zeros((32, rows), BF)], 0).T
    link = side[:, LINK : LINK + 1]
    kept_rows = side[:, KEEP : KEEP + 1].astype(F32)
    xe[:, 0:512] = x[...]
    xe[0:ROWS, 512:1024] = carry[...] * link[0:ROWS]
    if rows > ROWS:
        xe[ROWS:, 512:1024] = x[0 : rows - ROWS, :] * link[ROWS:]
    xe[:, 1024:1152] = side
    carry[...] = x[rows - ROWS :, :]

    size = rows // subs
    for s in range(subs):
        at = slice(s * size, (s + 1) * size)
        up_all = nt_dot(res[at, :], o[:, 0:512]) + nt_dot(skp[at, :], o[:, 512:1024])
        for n in range(2):
            base = n * 2 * half
            pre = dot(xe[at, :], w[:, base : base + 2 * half])
            up = up_all[:, n * half : (n + 1) * half]
            filt = jnp.tanh(pre[:, :half])
            gate = 0.5 * jnp.tanh(0.5 * pre[:, half:]) + 0.5
            kept = kept_rows[at] * gate
            hidden = filt * kept
            hid[at, n * half : (n + 1) * half] = hidden.astype(BF)
            p[at, base : base + half] = (up * kept * (1.0 - filt * filt)).astype(BF)
            p[at, base + half : base + 2 * half] = (up * hidden * (1.0 - gate)).astype(BF)
    acc[...] += tn_dot(xe[...], p[...])
    left = jnp.concatenate([hid[...], side[:, MEL : MEL + TILE]], 1)
    got = tn_dot(left, jnp.concatenate([res[...], skp[...]], 1))
    acc_out[...] += got[0:512]
    sums[...] += got[512:520]

    @pl.when(step == 0)
    def _():
        past = nt_dot(p[0:ROWS, :], w[512:1024, :])
        edge[...] = (past * link[0:ROWS].astype(F32)).astype(BF)

    @pl.when(step == last)
    def _():
        if not split:
            grad[...] = acc[...]
            grad_out[...] = acc_out[...]
            return
        for copy in passed:
            copy.wait()
        small[...] = jnp.zeros_like(small)
        for s in range(8):
            lane = mixed_block(s) * LANES
            small[s, 0:MEL, :] = acc[1024 : 1024 + MEL, lane : lane + LANES]
            for e in range(2):
                if s < 4:
                    lane = mixed_block(2 * s + e) * LANES
                    line = acc[1024 + ONES : 1024 + ONES + 1, lane : lane + LANES]
                else:
                    lane = (2 * (s - 4) + e) * LANES
                    line = sums[0:1, lane : lane + LANES]
                small[s, MEL + e : MEL + e + 1, :] = line

        def write(dest, shard, quarter):
            row = pl.multiple_of(64 * shard + TILE * quarter, TILE)
            put_tiles(dest, 0, acc[pl.ds(row, TILE), :], mixed_block)
            put_tiles(dest, 128, acc[pl.ds(512 + row, TILE), :], mixed_block)
            at = pl.multiple_of(32 * quarter, 32)
            dest[256:GATE_PART, :] = small[shard, pl.ds(at, 32), :].astype(dest.dtype)
            put_tiles(dest, GATE_PART, acc_out[pl.ds(row, TILE), :])

        emit_pieces((keep_out, send_out), write)


def gates_layer(split, rows, subs, x, tail, mel, flags, res, skp, extra):
    total = x.shape[0]
    steps = total // rows
    by_row = lambda columns: pl.BlockSpec((rows, columns), lambda i: (i, 0))
    by_lane = lambda high: pl.BlockSpec((high, rows), lambda i: (0, i))
    in_specs = [
        by_row(512),
        whole((ROWS, 512)),
        by_lane(MEL),
        by_lane(TILE),
        by_row(512),
        by_row(512),
    ] + [ANY if split else whole(e.shape) for e in extra]
    out_specs = [
        by_row(1024),
        by_row(512),
        whole((ROWS, 512)),
    ]
    out_shape = [
        jax.ShapeDtypeStruct((total, 1024), BF),
        jax.ShapeDtypeStruct((total, 512), BF),
        jax.ShapeDtypeStruct((ROWS, 512), BF),
    ]
    if split:
        more = [
            ((8, 1024), F32),
            ((4, 4, PART, LANES), BF),
            ((4, 4, PART, LANES), BF),
        ]
    else:
        more = [((1024 + AUX, 1024), F32), ((512, 1024), F32), ((8, 1024), F32)]
    if split:
        for shape in ((1024 + AUX, 1024), (512, 1024)):
            out_specs.append(ANY)
            out_shape.append(jax.ShapeDtypeStruct(shape, BF))
    for shape, dtype in more:
        out_specs.append(whole(shape))
        out_shape.append(jax.ShapeDtypeStruct(shape, dtype))
    scratch = [
        pltpu.VMEM((rows, 1024 + AUX), BF),
        pltpu.VMEM((ROWS, 512), BF),
        pltpu.VMEM((1024 + AUX, 1024), F32),
        pltpu.VMEM((512, 1024), F32),
    ]
    if split:
        scratch += [
            pltpu.VMEM((8, 1024), F32),
            pltpu.VMEM((8, AUX, LANES), F32),
            pltpu.VMEM((8, AUX, LANES), BF),
            pltpu.VMEM((1024 + AUX, 1024), BF),
            pltpu.VMEM((512, 1024), BF),
            pltpu.SemaphoreType.DMA((12,)),
        ]
        scratch += [pltpu.VMEM(e.shape, e.dtype) for e in extra]
    return pl.pallas_call(
        functools.partial(gates_body, split, subs),
        grid=(steps,),
        in_specs=in_specs,
        out_specs=out_specs,
        out_shape=out_shape,
        scratch_shapes=scratch,
        compiler_params=params(GATES_MIB),
        cost_estimate=cost(6.75 * 2 * total * 512 * 1024, total * 8000),
        name="gates_layer",
    )(x, tail, mel, flags, res, skp, *extra)


def mixed_body(x, hid, o, bias, *refs):
    residual, skip, token = refs[-3:]
    mixed = dot(hid[...], o[...]) + bias[0:1, :]
    residual[...] = (x[...].astype(F32) + mixed[:, 0:512]).astype(BF)
    skip[...] = mixed[:, 512:1024].astype(BF)

    @pl.when(pl.program_id(0) == 0)
    def _():
        token[...] = jnp.zeros_like(token)


def patch_body(x, hid, o, bias, rest, edge, *refs):
    residual, skip, patch, token = refs[-4:]
    mixed_body(x, hid, o, bias, residual, skip, token)

    @pl.when(pl.program_id(0) == 0)
    def _():
        patch[...] = (rest[...] + edge[...].astype(F32)).astype(BF)


def mixed_layer(rows, first, steps, x, hid, o, bias, patched, partial, after):
    total = x.shape[0]
    by_row = pl.BlockSpec((rows, 512), lambda i: (first + i, 0))
    last = pl.BlockSpec((ROWS, 512), lambda i: (total // ROWS - 1, 0))
    operands = [x, hid, o, bias]
    in_specs = [by_row, by_row, whole((512, 1024)), whole((8, 1024))]
    out_specs = [by_row, by_row]
    aliases = {}
    if patched:
        rest, edge, input_grad = patched
        operands += [rest, edge, input_grad]
        in_specs += [whole((ROWS, 512)), whole((ROWS, 512)), ANY]
        out_specs.append(last)
        aliases[6] = 2
    for n, array in enumerate(partial):
        aliases[len(operands)] = n
        operands.append(array)
        in_specs.append(ANY)
    return pl.pallas_call(
        patch_body if patched else mixed_body,
        grid=(steps,),
        in_specs=in_specs + [ANY] * len(after),
        out_specs=out_specs + [whole(TOKEN.shape)],
        out_shape=[jax.ShapeDtypeStruct((total, 512), BF)] * len(out_specs) + [TOKEN],
        input_output_aliases=aliases,
        compiler_params=params(58),
        cost_estimate=cost(2 * rows * steps * 512 * 1024, rows * steps * 4096),
        name="mixed_layer_%d" % first,
    )(*operands, *after)


def input_body(res, p, flags, w, *refs):
    out, rest, token, carry = refs[-4:]
    step = pl.program_id(0)
    rows = res.shape[0]
    link = flags[...].T[:, LINK - MEL : LINK - MEL + 1].astype(F32)
    both = nt_dot(p[...], w[...])
    past = both[:, 512:1024] * link
    now = res[...].astype(F32) + both[:, 0:512]

    @pl.when(step == 0)
    def _():
        rest[...] = now[rows - ROWS :]
        carry[...] = jnp.zeros_like(carry)
        token[...] = jnp.zeros_like(token)

    if rows > ROWS:
        out[0 : rows - ROWS, :] = (now[0 : rows - ROWS] + past[ROWS:]).astype(BF)
    out[rows - ROWS :, :] = (now[rows - ROWS :] + carry[...]).astype(BF)
    carry[...] = past[0:ROWS]


def input_layer(rows, res, p, flags, w, after):
    total = res.shape[0]
    steps = total // rows
    by_row = lambda columns: pl.BlockSpec((rows, columns), lambda i: (steps - 1 - i, 0))
    return pl.pallas_call(
        input_body,
        grid=(steps,),
        in_specs=[
            by_row(512),
            by_row(1024),
            pl.BlockSpec((TILE, rows), lambda i: (0, steps - 1 - i)),
            pl.BlockSpec((1024, 1024), lambda i: (0, 0)),
        ]
        + [ANY] * len(after),
        out_specs=[by_row(512), whole((ROWS, 512)), whole(TOKEN.shape)],
        out_shape=[
            jax.ShapeDtypeStruct((total, 512), BF),
            jax.ShapeDtypeStruct((ROWS, 512), F32),
            TOKEN,
        ],
        scratch_shapes=[pltpu.VMEM((ROWS, 512), F32)],
        compiler_params=params(58),
        cost_estimate=cost(4 * total * 512 * 1024, total * 4096),
        name="input_layer",
    )(res, p, flags, w, *after)


def cores_body(keep, got, *outs):
    for n in range(4):
        outs[n][...] = (keep[n].astype(F32) + got[n].astype(F32)).astype(outs[n].dtype)


def add_cores(keep, got):
    spec = pl.BlockSpec((4, 1, PART, LANES), lambda i: (0, i, 0, 0))
    return pl.pallas_call(
        cores_body,
        grid=(4,),
        in_specs=[spec, spec],
        out_specs=[pl.BlockSpec((1, PART, LANES), lambda i: (i, 0, 0))] * 4,
        out_shape=[jax.ShapeDtypeStruct((4, PART, LANES), BF if n else F32) for n in range(4)],
        compiler_params=params(),
        cost_estimate=cost(10**6, 8 * 10**6),
        name="add_cores",
    )(keep, got)


def hop_body(keep, g1, g2, g3, *refs):
    outs = refs[-5:]
    outs[4][...] = jnp.zeros_like(outs[4])
    for n in range(4):
        total = keep[n] + g1[n].astype(F32) + g2[n].astype(F32) + g3[n].astype(F32)
        outs[n][...] = total.astype(outs[n].dtype)


def add_hop(parts, after):
    return pl.pallas_call(
        hop_body,
        in_specs=[VMEM] * 4 + [ANY] * len(after),
        out_specs=[VMEM] * 5,
        out_shape=[jax.ShapeDtypeStruct((PART, LANES), BF if n else F32) for n in range(4)] + [TOKEN],
        compiler_params=params(),
        cost_estimate=cost(10**6, 3 * 10**6),
        name="add_hop",
    )(*parts, *after)


def last_body(keep, g1, g2, g3, *refs):
    total, square = refs[-2:]
    total[...] = keep[...] + g1[...].astype(F32) + g2[...].astype(F32) + g3[...].astype(F32)
    square[...] = jnp.full(square.shape, jnp.sum(total[...] * total[...]), F32)


def add_last(parts, devices, after):
    return pl.pallas_call(
        last_body,
        in_specs=[VMEM] * 4 + [ANY] * len(after),
        out_specs=[VMEM] * 2,
        out_shape=[
            jax.ShapeDtypeStruct((PART, LANES), F32),
            jax.ShapeDtypeStruct((devices, LANES), F32),
        ],
        compiler_params=params(),
        cost_estimate=cost(10**6, 10**6),
        name="add_last",
    )(*parts, *after)


def adamw_update(grad, moment, second, weight, factor, decay):
    clipped = grad * factor
    moment_new = beta_one * moment + (1.0 - beta_one) * clipped
    second_new = beta_two * second + (1.0 - beta_two) * clipped * clipped
    mean_hat = moment_new / (1.0 - beta_one**STEP)
    square_hat = second_new / (1.0 - beta_two**STEP)
    weight_new = weight - learn_rate * (
        mean_hat / (jnp.sqrt(square_hat) + epsilon) + decay * weight
    )
    return (moment_new, second_new, weight_new)


def update_body(*refs):
    squares, parts = refs[0], refs[1:5]
    conv, cond, out, bias = refs[5:8], refs[8:11], refs[11:14], refs[14:17]
    norm, new, small = refs[17], refs[18:30], refs[30]
    _, rep, _ = spot()
    grad_norm = jnp.sqrt(jnp.sum(squares[...], 0, keepdims=True))
    norm[...] = grad_norm
    factor = clip_bound / jnp.maximum(grad_norm, clip_bound)

    def step(grad, old, dest, at, decay):
        got = adamw_update(grad, *[ref[at] for ref in old], factor, decay)
        for ref, value in zip(dest, got):
            ref[at] = value

    for k in range(4):
        row = pl.multiple_of((rep ^ k) * TILE, TILE)
        for b in range(8):
            lanes = slice(b * LANES, (b + 1) * LANES)
            for t in range(2):
                base = t * 128 + b * TILE
                step(parts[k][base : base + TILE, :], conv, new[0:3], (pl.ds(row, TILE), t, lanes), weight_decay)
            base = GATE_PART + b * TILE
            step(parts[k][base : base + TILE, :], out, new[6:9], (pl.ds(row, TILE), lanes), weight_decay)
        small[pl.ds(2 * row, 32), :] = parts[k][256:GATE_PART, :]
    step(small[0:MEL, :], cond, new[3:6], (slice(0, MEL), slice(0, LANES)), weight_decay)
    step(small[MEL : MEL + 2, :], bias, new[9:12], (slice(0, 2), slice(0, LANES)), 0.0)


def update(squares, parts, conv, cond, out, bias):
    shapes = [(1, LANES)]
    for group in (conv, cond, out, bias):
        shapes += [group[0].shape] * 3
    return pl.pallas_call(
        update_body,
        in_specs=[VMEM] * 17,
        out_specs=[VMEM] * 13,
        out_shape=[jax.ShapeDtypeStruct(s, F32) for s in shapes],
        scratch_shapes=[pltpu.VMEM((AUX, LANES), F32)],
        compiler_params=params(),
        name="update",
    )(squares, *parts, *conv, *cond, *out, *bias)


def local(
    inputs,
    mel_frames,
    utterance,
    keep_mask,
    res_grad,
    skip_grad,
    conv_weight,
    cond_weight,
    out_weight,
    biases,
    conv_first,
    conv_second,
    cond_first,
    cond_second,
    out_first,
    out_second,
    bias_first,
    bias_second,
):
    rows, width = inputs.shape
    span = DILATION_STEP
    split = lax.axis_size("rep") == 4 and lax.axis_size("seq") == 8
    tile = 1024

    if split:
        own, first = pack_weights(conv_weight, cond_weight, biases.reshape(2, LANES), out_weight)
        along = [swap(first, 0, 2 * j) for j in (1, 2, 3)]
        tail = from_behind(last_rows(inputs, along[0]), BOTH, 1)
        stack = jnp.concatenate(along, 0)
        parts = across_hops(own, stack)
    else:
        w, o, bias_out = gather_plain(conv_weight, out_weight, cond_weight, biases)
        tail = from_behind(inputs[rows - span :], BOTH, 1)

    tail_ids = from_behind(utterance[rows - span :], BOTH, 1)
    flags = flag_rows(
        keep_mask.reshape(1, rows), utterance.reshape(1, rows), tail_ids.reshape(1, span), tail
    )
    samples = (inputs, tail, mel_frames, flags, res_grad, skip_grad)
    if split:
        p, hid, edge, w, o, bias_out, keep, send = gates_layer(split, tile, 2, *samples, parts)
        got = add_cores(keep, swap(send, 0, 1))
        part = [got[0]] + [swap(got[n], n, 0) for n in (1, 2, 3)]
        after = (got[1],)
    else:
        p, hid, edge, grad, grad_out, sums = gates_layer(split, tile, 2, *samples, (w, o))
        after = ()

    returned = from_behind(edge, BOTH, -1)
    input_grad, rest, token = input_layer(tile, res_grad, p, flags, w, after)
    if split:
        got = add_hop(part, (token,))
        part = [got[0]] + [swap(got[n], 0, 2 * n) for n in (1, 2, 3)]
        after = (got[4],)
    steps = rows // tile
    cut = steps * 4 // 6
    mixed = functools.partial(mixed_layer, tile)
    *sample_outs, token = mixed(0, cut, inputs, hid, o, bias_out, (), (), after)
    if split:
        total, square = add_last(part, lax.axis_size(BOTH), (token,))
        after = (square,)
    residual_out, skip_out, input_grad, _ = mixed(
        cut, steps - cut, inputs, hid, o, bias_out, (rest, returned, input_grad), sample_outs, after
    )

    if split:
        part = [total] + [swap(total, n, 0) for n in (1, 2, 3)]
        squares = lax.all_to_all(square, BOTH, 0, 0, tiled=True)
        fold = lambda v: v.reshape(2, LANES)
        norm, *new = update(
            squares,
            part,
            (conv_first, conv_second, conv_weight),
            (cond_first, cond_second, cond_weight),
            (out_first, out_second, out_weight),
            (fold(bias_first), fold(bias_second), fold(biases)),
        )
        grad_norm = norm[0, 0]
        new = new[:9] + [v.reshape(-1) for v in new[9:]]
    else:
        grad = mixed_columns(grad)
        grad_conv = jnp.stack([grad[0:512], grad[512:1024]], 1)
        grad_bias = jnp.concatenate([grad[1024 + ONES], sums[0]], 0)
        own = (
            lax.psum_scatter(grad_conv, "seq", scatter_dimension=0, tiled=True),
            lax.psum_scatter(grad[1024 : 1024 + MEL], "seq", scatter_dimension=1, tiled=True),
            lax.psum_scatter(grad_out, "seq", scatter_dimension=0, tiled=True),
            lax.psum_scatter(grad_bias, "seq", scatter_dimension=0, tiled=True),
        )
        own = lax.psum(own, "rep")
        grad_norm = jnp.sqrt(lax.psum(sum(jnp.sum(g * g) for g in own), "seq"))
        factor = clip_bound / jnp.maximum(grad_norm, clip_bound)
        new = [
            *adamw_update(own[0], conv_first, conv_second, conv_weight, factor, weight_decay),
            *adamw_update(own[1], cond_first, cond_second, cond_weight, factor, weight_decay),
            *adamw_update(own[2], out_first, out_second, out_weight, factor, weight_decay),
            *adamw_update(own[3], bias_first, bias_second, biases, factor, 0.0),
        ]
    return (residual_out, skip_out, input_grad, grad_norm, *new)


def solution(mesh):
    rows = P(BOTH, None)
    line = P(BOTH)
    conv = P("seq", None, None)
    cond = P(None, "seq")
    out = P("seq", None)
    bias = P("seq")
    placed = (
        rows,
        P(None, BOTH),
        line,
        line,
        rows,
        rows,
        conv,
        cond,
        out,
        bias,
        conv,
        conv,
        cond,
        cond,
        out,
        out,
        bias,
        bias,
    )
    return jax.shard_map(
        local,
        mesh=mesh,
        in_specs=placed,
        out_specs=(rows, rows, rows, P()) + (conv,) * 3 + (cond,) * 3 + (out,) * 3 + (bias,) * 3,
        check_vma=False,
    )
```
